128 devices in a mesh: seq: 8 (over y_hi, x), res: 16 (over z, y_lo, core).
Axes of the slice: x: 4, y: 4 (y_hi: 2, y_lo: 2; y = y_hi * 2 + y_lo), z: 4, core: 2. Of those that a mesh axis runs over, the one named last changes fastest.
Arguments:
- homolog_tensor: bfloat16 [128, 2048, 256], P('seq', 'res'), may hold values from -3 to 3
- horizontal_probe_matrix: bfloat16 [256, 256], replicated, may hold values from -3 to 3, as said below
- horizontal_lookup_matrix: bfloat16 [256, 256], replicated, may hold values from -3 to 3, as said below
- horizontal_payload_matrix: bfloat16 [256, 256], replicated, may hold values from -0.375 to 0.375
- horizontal_sigmoid_matrix: bfloat16 [256, 256], replicated, may hold values from -0.375 to 0.375
- horizontal_final_matrix: bfloat16 [256, 256], replicated, may hold values from -0.375 to 0.375
- vertical_probe_matrix: bfloat16 [256, 256], replicated, may hold values from -3 to 3, as said below
- vertical_lookup_matrix: bfloat16 [256, 256], replicated, may hold values from -3 to 3, as said below
- vertical_payload_matrix: bfloat16 [256, 256], replicated, may hold values from -0.375 to 0.375
- vertical_sigmoid_matrix: bfloat16 [256, 256], replicated, may hold values from -0.375 to 0.375
- vertical_final_matrix: bfloat16 [256, 256], replicated, may hold values from -0.375 to 0.375
- expanding_matrix: bfloat16 [256, 1024], replicated, may hold values from -0.375 to 0.375
- shrinking_matrix: bfloat16 [1024, 256], replicated, may hold values from -0.1875 to 0.1875
Outputs:
- refreshed_homologs: bfloat16 [128, 2048, 256], P('seq', 'res')
The draws below stay inside these ranges and needn't reach their ends.
Inputs may be any that keep to these rules, and one draw needn't show every extreme that they name: `horizontal_probe_matrix`: entries of a projection matrix. `horizontal_lookup_matrix`: entries of a projection matrix. `vertical_probe_matrix`: entries of a projection matrix. `vertical_lookup_matrix`: entries of a projection matrix.
All inputs are finite; a program needn't handle non-finite values.
Results may differ from the reference program's by a relative error of at most 0.023.
Values may be sent and summed in bfloat16 or wider, within the bound.
A program may use at most 128 MiB of HBM per device.

```python
import math
import jax
import jax.numpy as jnp
from jax import lax

FEATURE_DEPTH = 256
HEADS = 8
HEAD_DIM = 32
EXPANSION_UNITS = 1024
HOMOLOG_TOTAL = 128
POSITION_TOTAL = 2048


def paired(key, random_offset):
    key = jax.random.fold_in(key, random_offset)
    leading_factor = jnp.clip(jax.random.normal(jax.random.fold_in(key, 1), (FEATURE_DEPTH, FEATURE_DEPTH), jnp.float32), -6.0, 6.0)
    trailing_factor = jnp.clip(jax.random.normal(jax.random.fold_in(key, 2), (FEATURE_DEPTH, FEATURE_DEPTH), jnp.float32), -6.0, 6.0)
    return (leading_factor, trailing_factor)


def draw_homolog_tensor(key, part):
    key = jax.random.fold_in(key, 100)
    sample_entries = 0.5 * jax.random.normal(jax.random.fold_in(key, 1), (HOMOLOG_TOTAL, POSITION_TOTAL, FEATURE_DEPTH), jnp.float32)
    return jnp.clip(sample_entries, -3.0, 3.0).astype(jnp.bfloat16)


def draw_horizontal_probe_matrix(key, part):
    leading_factor, trailing_factor = paired(key, 11)
    return (leading_factor * 1.8 * FEATURE_DEPTH ** (-0.5)).astype(jnp.bfloat16)


def draw_horizontal_lookup_matrix(key, part):
    leading_factor, trailing_factor = paired(key, 11)
    return (trailing_factor * 1.8 * FEATURE_DEPTH ** (-0.5)).astype(jnp.bfloat16)


def draw_vertical_probe_matrix(key, part):
    leading_factor, trailing_factor = paired(key, 12)
    return (leading_factor * 1.8 * FEATURE_DEPTH ** (-0.5)).astype(jnp.bfloat16)


def draw_vertical_lookup_matrix(key, part):
    leading_factor, trailing_factor = paired(key, 12)
    return (trailing_factor * 1.8 * FEATURE_DEPTH ** (-0.5)).astype(jnp.bfloat16)


def noise(key, extent, scale, most, dtype=jnp.bfloat16):
    entries = jax.random.normal(key, extent, jnp.float32) * scale
    return jnp.minimum(jnp.maximum(entries, -most), most).astype(dtype)


def setup_inputs(seed: int = 0) -> dict:
    key_list = jax.random.split(jax.random.key(seed), 14)
    return {
        "homolog_tensor": draw_homolog_tensor(jax.random.fold_in(key_list[13], 71), 0),
        "horizontal_probe_matrix": draw_horizontal_probe_matrix(jax.random.fold_in(key_list[13], 71), 0),
        "horizontal_lookup_matrix": draw_horizontal_lookup_matrix(jax.random.fold_in(key_list[13], 71), 0),
        "horizontal_payload_matrix": noise(key_list[3], (FEATURE_DEPTH, FEATURE_DEPTH), FEATURE_DEPTH ** -0.5, 0.375),
        "horizontal_sigmoid_matrix": noise(key_list[4], (FEATURE_DEPTH, FEATURE_DEPTH), FEATURE_DEPTH ** -0.5, 0.375),
        "horizontal_final_matrix": noise(key_list[5], (FEATURE_DEPTH, FEATURE_DEPTH), FEATURE_DEPTH ** -0.5, 0.375),
        "vertical_probe_matrix": draw_vertical_probe_matrix(jax.random.fold_in(key_list[13], 71), 0),
        "vertical_lookup_matrix": draw_vertical_lookup_matrix(jax.random.fold_in(key_list[13], 71), 0),
        "vertical_payload_matrix": noise(key_list[8], (FEATURE_DEPTH, FEATURE_DEPTH), FEATURE_DEPTH ** -0.5, 0.375),
        "vertical_sigmoid_matrix": noise(key_list[9], (FEATURE_DEPTH, FEATURE_DEPTH), FEATURE_DEPTH ** -0.5, 0.375),
        "vertical_final_matrix": noise(key_list[10], (FEATURE_DEPTH, FEATURE_DEPTH), FEATURE_DEPTH ** -0.5, 0.375),
        "expanding_matrix": noise(key_list[11], (FEATURE_DEPTH, EXPANSION_UNITS), FEATURE_DEPTH ** -0.5, 0.375),
        "shrinking_matrix": noise(key_list[12], (EXPANSION_UNITS, FEATURE_DEPTH), EXPANSION_UNITS ** -0.5, 0.1875),
    }


def layer_normalize(sample_entries):
    center = sample_entries - lax.optimization_barrier(jnp.mean(sample_entries, axis=-1, keepdims=True))
    spread = lax.optimization_barrier(jnp.mean(center * center, axis=-1, keepdims=True))
    return center * lax.rsqrt(spread + 1e-05)

def softmax_last(sample_entries):
    highest = lax.optimization_barrier(jnp.max(sample_entries, axis=-1, keepdims=True))
    expo = jnp.exp(sample_entries - highest)
    return expo / lax.optimization_barrier(jnp.sum(expo, axis=-1, keepdims=True))

def linear_project(inputs, weight):
    return jnp.dot(inputs, weight, preferred_element_type=jnp.float32)

def reference(homolog_tensor, horizontal_probe_matrix, horizontal_lookup_matrix, horizontal_payload_matrix, horizontal_sigmoid_matrix, horizontal_final_matrix, vertical_probe_matrix, vertical_lookup_matrix, vertical_payload_matrix, vertical_sigmoid_matrix, vertical_final_matrix, expanding_matrix, shrinking_matrix):
    merged_homologs = homolog_tensor.astype(jnp.float32).reshape(HOMOLOG_TOTAL * POSITION_TOTAL, FEATURE_DEPTH)
    normalized_input = layer_normalize(merged_homologs).astype(jnp.bfloat16)
    row_q = linear_project(normalized_input, horizontal_probe_matrix).astype(jnp.bfloat16).reshape(HOMOLOG_TOTAL, POSITION_TOTAL, HEADS, HEAD_DIM)
    row_k = linear_project(normalized_input, horizontal_lookup_matrix).astype(jnp.bfloat16).reshape(HOMOLOG_TOTAL, POSITION_TOTAL, HEADS, HEAD_DIM)
    horizontal_payload = linear_project(normalized_input, horizontal_payload_matrix).astype(jnp.bfloat16).reshape(HOMOLOG_TOTAL, POSITION_TOTAL, HEADS, HEAD_DIM)
    row_g = jax.nn.sigmoid(linear_project(normalized_input, horizontal_sigmoid_matrix))
    tied = jnp.einsum('sihd,sjhd->hij', row_q.astype(jnp.float32), row_k.astype(jnp.float32))
    tied = tied * (1.0 / math.sqrt(HOMOLOG_TOTAL * HEAD_DIM))
    horizontal_probabilities = softmax_last(tied).astype(jnp.bfloat16)
    horizontal_result = jnp.einsum('pmn,qnpc->qmpc', horizontal_probabilities.astype(jnp.float32), horizontal_payload.astype(jnp.float32)).reshape(HOMOLOG_TOTAL * POSITION_TOTAL, FEATURE_DEPTH)
    row_delta = (row_g * horizontal_result).astype(jnp.bfloat16)
    row_updated = (merged_homologs + linear_project(row_delta, horizontal_final_matrix)).astype(jnp.bfloat16)
    normed_col = layer_normalize(row_updated.astype(jnp.float32)).astype(jnp.bfloat16)
    col_q = linear_project(normed_col, vertical_probe_matrix).astype(jnp.bfloat16).reshape(HOMOLOG_TOTAL, POSITION_TOTAL, HEADS, HEAD_DIM)
    col_k = linear_project(normed_col, vertical_lookup_matrix).astype(jnp.bfloat16).reshape(HOMOLOG_TOTAL, POSITION_TOTAL, HEADS, HEAD_DIM)
    vertical_payload = linear_project(normed_col, vertical_payload_matrix).astype(jnp.bfloat16).reshape(HOMOLOG_TOTAL, POSITION_TOTAL, HEADS, HEAD_DIM)
    col_g = jax.nn.sigmoid(linear_project(normed_col, vertical_sigmoid_matrix))
    scores = jnp.einsum('snhd,tnhd->nhst', col_q.astype(jnp.float32), col_k.astype(jnp.float32))
    vertical_probabilities = softmax_last(scores * (1.0 / math.sqrt(HEAD_DIM))).astype(jnp.bfloat16)
    vertical_result = jnp.einsum('kmpv,vkml->pkml', vertical_probabilities.astype(jnp.float32), vertical_payload.astype(jnp.float32)).reshape(HOMOLOG_TOTAL * POSITION_TOTAL, FEATURE_DEPTH)
    col_u = (col_g * vertical_result).astype(jnp.bfloat16)
    column_updated = (row_updated.astype(jnp.float32) + linear_project(col_u, vertical_final_matrix)).astype(jnp.bfloat16)
    normed_tr = layer_normalize(column_updated.astype(jnp.float32)).astype(jnp.bfloat16)
    hidden_state = jax.nn.relu(linear_project(normed_tr, expanding_matrix)).astype(jnp.bfloat16)
    refreshed_homologs = (column_updated.astype(jnp.float32) + linear_project(hidden_state, shrinking_matrix)).astype(jnp.bfloat16)
    return refreshed_homologs.reshape(HOMOLOG_TOTAL, POSITION_TOTAL, FEATURE_DEPTH)
```

```python
import math

import jax
import jax.numpy as jnp
from jax import lax
from jax.experimental import pallas as pl
from jax.experimental.pallas import tpu as pltpu
from jax.sharding import PartitionSpec as P

HEADS = 8
HEAD_DIM = 32
SEQ_DEVICES = 8
MESH = pl.DeviceIdType.MESH
BF16 = jnp.bfloat16
F32 = jnp.float32
NT = (((1,), (1,)), ((), ()))


def layer_normalize(entries):
    center = entries - jnp.mean(entries, axis=-1, keepdims=True)
    spread = jnp.mean(center * center, axis=-1, keepdims=True)
    return center * lax.rsqrt(spread + 1e-05)


def matmul(a, b):
    return jnp.dot(a, b, preferred_element_type=F32)


def matmul_nt(a, b):
    return lax.dot_general(a, b, NT, preferred_element_type=F32)


def flip(a):
    return a.astype(F32).T.astype(BF16)


def remote(src, dst, send, recv, device):
    return pltpu.make_async_remote_copy(
        src_ref=src, dst_ref=dst, send_sem=send, recv_sem=recv, device_id=device, device_id_type=MESH
    )


def row_kernel(
    x, wq, wk, wv, wg, wf, out,
    normed, wt, ks, qs, vs, kz, vz, qg, logits, probs, gates, stats,
    o_part, oc_s, oc_r, oy_s, oy_r, oa_s, ob, after,
    ka_s, ka_r, qa_s, qa_r, va_s, va_r, kz_s, kz_r, vz_s, vz_r, qp_s, qp_r,
    st_s, st_r, oc_ss, oc_rs, oy_ss, oy_rs, oa_ss, oa_rs, col_s, col_r, own_s,
):
    me = lax.axis_index("seq")
    res = lax.axis_index("res")
    z = res // 4
    yl = lax.rem(res // 2, 2)
    c = lax.rem(res, 2)
    here = lax.rem(res, 4)

    def at_res(zz, yy, cc):
        return (me, zz * 4 + yy * 2 + cc)

    z_up = lax.rem(z + 1, 4)
    z_down = lax.rem(z + 3, 4)
    z_far = lax.rem(z + 2, 4)
    up = at_res(z_up, yl, c)
    down = at_res(z_down, yl, c)
    twin = at_res(z, yl, 1 - c)
    beside = at_res(z, 1 - yl, c)
    across = at_res(z, 1 - yl, 1 - c)

    def ahead(t):
        return lax.rem(me + t, SEQ_DEVICES)

    def behind(t):
        return lax.rem(me + SEQ_DEVICES - t, SEQ_DEVICES)

    barrier = pltpu.get_barrier_semaphore()
    partners = [(ahead(t), res) for t in range(1, SEQ_DEVICES)] + [up, down, twin, beside, across]
    for device in partners:
        pl.semaphore_signal(barrier, inc=1, device_id=device, device_id_type=MESH)
    pl.semaphore_wait(barrier, len(partners))

    wt[0:256, :] = flip(wk[...])
    wt[256:512, :] = flip(wq[...])
    wt[512:768, :] = flip(wv[...])
    wt[768:1024, :] = flip(wg[...])
    logits[...] = jnp.zeros_like(logits)

    @pl.loop(0, 4)
    def _(quad):
        rows = pl.ds(pl.multiple_of(quad * 512, 512), 512)
        part = layer_normalize(x[rows, :].astype(F32)).astype(BF16)
        normed[rows, :] = part
        keys = matmul_nt(wt[0:256, :], part)
        lanes = pl.ds(pl.multiple_of(quad * 128, 128), 128)
        for h in range(HEADS):
            block = keys[32 * h : 32 * h + 32, :]
            stack = jnp.concatenate([block[:, 128 * s : 128 * s + 128] for s in range(4)], axis=0)
            ks[h, :, lanes] = stack.T.astype(BF16)

    def ka(t):
        return remote(ks.at[behind(t)], kz.at[z, me], ka_s.at[t], ka_r.at[t], (behind(t), res))

    def qa(t):
        return remote(qs.at[behind(t)], qg.at[here, me], qa_s.at[t], qa_r.at[t], (behind(t), res))

    def va(t):
        return remote(vs.at[behind(t)], vz.at[z, me], va_s.at[t], va_r.at[t], (behind(t), res))

    own_k = pltpu.make_async_copy(ks.at[me], kz.at[z, me], own_s.at[0])
    own_q = pltpu.make_async_copy(qs.at[me], qg.at[here, me], own_s.at[1])
    own_v = pltpu.make_async_copy(vs.at[me], vz.at[z, me], own_s.at[2])
    own_k.start()
    for t in range(1, SEQ_DEVICES):
        ka(t).start()

    @pl.loop(0, 4)
    def _(quad):
        rows = pl.ds(pl.multiple_of(quad * 512, 512), 512)
        both = matmul_nt(wt[256:768, :], normed[rows, :]).astype(BF16)
        for h in range(HEADS):
            for s in range(4):
                place = pl.ds(pl.multiple_of(quad * 128 + 32 * s, 32), 32)
                lanes = slice(128 * s, 128 * s + 128)
                qs[h, place, :] = both[32 * h : 32 * h + 32, lanes]
                vs[h, place, :] = both[256 + 32 * h : 256 + 32 * h + 32, lanes]

    own_q.start()
    own_v.start()

    def ring(buf, send, recv, t):
        g = ahead(t)
        return (
            remote(buf.at[z, g], buf.at[z, g], send.at[0, t], recv.at[0, t], up),
            remote(buf.at[z, g], buf.at[z, g], send.at[1, t], recv.at[1, t], down),
        )

    def ring_arrived(buf, send, recv, t):
        g = ahead(t)
        remote(buf.at[z_down, g], buf.at[z_down, g], send.at[0, t], recv.at[0, t], up).wait_recv()
        remote(buf.at[z_up, g], buf.at[z_up, g], send.at[1, t], recv.at[1, t], down).wait_recv()

    def onward_up(buf, send, recv, t):
        g = ahead(t)
        return remote(buf.at[z_down, g], buf.at[z_down, g], send.at[2, t], recv.at[2, t], up)

    def onward_down(buf, send, recv, t):
        g = ahead(t)
        return remote(buf.at[z_up, g], buf.at[z_up, g], send.at[2, t], recv.at[2, t], down)

    def far_arrived(buf, send, recv, t):
        g = ahead(t)
        remote(buf.at[z_far, g], buf.at[z_far, g], send.at[2, t], recv.at[2, t], up).wait_recv()

    def ring_forward(buf, send, recv, t):
        ring_arrived(buf, send, recv, t)

        @pl.when(lax.rem(t, 2) == 0)
        def _():
            onward_up(buf, send, recv, t).start()

        @pl.when(lax.rem(t, 2) == 1)
        def _():
            onward_down(buf, send, recv, t).start()

    kzs = (kz, kz_s, kz_r)
    vzs = (vz, vz_s, vz_r)

    here_twin = yl * 2 + (1 - c)
    here_beside = (1 - yl) * 2 + c
    here_across = (1 - yl) * 2 + (1 - c)

    def q_twin(t):
        g = ahead(t)
        return remote(qg.at[here, g], qg.at[here, g], qp_s.at[0, t], qp_r.at[0, t], twin)

    def q_beside(t):
        g = ahead(t)
        return remote(qg.at[here, g], qg.at[here, g], qp_s.at[1, t], qp_r.at[1, t], beside)

    def q_onward(t):
        g = ahead(t)
        return remote(qg.at[here_beside, g], qg.at[here_beside, g], qp_s.at[2, t], qp_r.at[2, t], twin)

    def q_arrived(slot, place, t):
        g = ahead(t)
        remote(qg.at[place, g], qg.at[place, g], qp_s.at[slot, t], qp_r.at[slot, t], twin).wait_recv()

    def add_logits(t):
        g = ahead(t)
        queries = jnp.concatenate([qg[p, g] for p in range(4)], axis=1)
        for zz in range(4):
            logits[128 * zz : 128 * zz + 128, :] += matmul(kz[zz, g], queries)

    scale = 1.0 / math.sqrt(SEQ_DEVICES * 16 * HEAD_DIM)

    def stat_copy(i, device):
        return remote(stats.at[here], stats.at[here], st_s.at[i], st_r.at[i], device)

    def stat_wait(i, place):
        remote(stats.at[place], stats.at[place], st_s.at[i], st_r.at[i], twin).wait_recv()

    def local_softmax():
        highest = jnp.max(logits[...], axis=0, keepdims=True)
        total = jnp.zeros((1, 512), F32)
        for zz in range(4):
            rows = slice(128 * zz, 128 * zz + 128)
            expo = jnp.exp((logits[rows, :] - highest) * scale)
            logits[rows, :] = expo
            total += jnp.sum(expo, axis=0, keepdims=True)
        stats[here, 0] = jnp.broadcast_to(highest, (8, 512))
        stats[here, 1] = jnp.broadcast_to(total, (8, 512))
        stat_copy(0, twin).start()
        stat_copy(1, beside).start()
        stat_copy(2, across).start()

    def finish_softmax():
        stat_wait(0, here_twin)
        stat_wait(1, here_beside)
        stat_wait(2, here_across)
        highest = stats[0, 0]
        for p in range(1, 4):
            highest = jnp.maximum(highest, stats[p, 0])
        total = jnp.zeros((8, 512), F32)
        for p in range(4):
            total += stats[p, 1] * jnp.exp((stats[p, 0] - highest) * scale)
        factor = jnp.exp((stats[here, 0] - highest) * scale) / total
        factor = factor[0:1, :]
        for zz in range(4):
            rows = slice(128 * zz, 128 * zz + 128)
            probs[rows, :] = (logits[rows, :] * factor).astype(BF16)

    def oc(t):
        return remote(oc_s.at[t], oc_r.at[t], oc_ss.at[t], oc_rs.at[t], twin)

    def oy(t):
        return remote(oy_s.at[t], oy_r.at[t], oy_ss.at[t], oy_rs.at[t], beside)

    def oa(t):
        return remote(oa_s.at[t], ob.at[me], oa_ss.at[t], oa_rs.at[t], (ahead(t), res))

    def attend(t):
        g = ahead(t)
        slot = lax.rem(t, 2)

        @pl.loop(0, 4)
        def _(rb):
            rows = pl.ds(pl.multiple_of(rb * 128, 128), 128)
            values = jnp.concatenate([vz[zz, g, rows, :] for zz in range(4)], axis=1)
            term = matmul(values, probs[...])
            for p in range(4):
                o_part[slot, p, rows, :] = term[:, 128 * p : 128 * p + 128]

        for y in range(2):
            oc_s[t, y] = o_part[slot, 2 * y + 1 - c].astype(BF16)
        oc(t).start()

    def add_twin(t):
        slot = lax.rem(t, 2)
        oc(t).wait_recv()
        oy_s[t] = (o_part[slot, here_beside] + oc_r[t, 1 - yl].astype(F32)).astype(BF16)
        oy(t).start()

    def add_beside(t):
        slot = lax.rem(t, 2)
        oy(t).wait_recv()
        total = o_part[slot, here] + oc_r[t, yl].astype(F32) + oy_r[t].astype(F32)

        @pl.when(t == 0)
        def _():
            ob[me] = total.astype(BF16)

        @pl.when(t > 0)
        def _():
            oa_s[t] = total.astype(BF16)
            oa(t).start()

    def gate_quad(quad):
        rows = pl.ds(pl.multiple_of(quad * 512, 512), 512)
        gate = jax.nn.sigmoid(matmul_nt(wt[768:1024, :], normed[rows, :]))
        for s in range(4):
            gates[quad * 4 + s] = gate[:, 128 * s : 128 * s + 128]

    @pl.loop(0, 24)
    def _(tick):
        def during(first, action, count=8):
            @pl.when((tick >= first) & (tick < first + count))
            def _():
                action(tick - first)

        def k_own(t):
            @pl.when(t == 0)
            def _():
                own_k.wait()

            @pl.when(t > 0)
            def _():
                remote(ks.at[0], kz.at[z, ahead(t)], ka_s.at[t], ka_r.at[t], (behind(t), res)).wait_recv()
                qa(t).start()

            for copy in ring(*kzs, t):
                copy.start()

        def q_peers(t):
            @pl.when(t == 0)
            def _():
                own_q.wait()

            @pl.when(t > 0)
            def _():
                remote(qs.at[0], qg.at[here, ahead(t)], qa_s.at[t], qa_r.at[t], (behind(t), res)).wait_recv()

            q_twin(t).start()
            q_beside(t).start()

        def q_forward(t):
            q_arrived(1, here_beside, t)
            q_onward(t).start()

        def v_send(t):
            @pl.when(t > 0)
            def _():
                va(t).start()

        def v_own(t):
            @pl.when(t == 0)
            def _():
                own_v.wait()

            @pl.when(t > 0)
            def _():
                remote(vs.at[0], vz.at[z, ahead(t)], va_s.at[t], va_r.at[t], (behind(t), res)).wait_recv()

            for copy in ring(*vzs, t):
                copy.start()

        def add_chunk(t):
            far_arrived(*kzs, t)
            q_arrived(0, here_twin, t)
            q_arrived(2, here_across, t)
            add_logits(t)

        def attend_chunk(t):
            far_arrived(*vzs, t)
            attend(t)

        during(16, add_beside)
        during(15, add_twin)
        during(0, k_own)
        during(8, v_own)
        during(2, lambda t: ring_forward(*kzs, t))
        during(10, lambda t: ring_forward(*vzs, t))
        during(2, q_peers)
        during(4, q_forward)
        during(3, v_send)
        during(3, gate_quad, 4)
        during(5, add_chunk)
        during(13, lambda t: local_softmax(), 1)
        during(14, lambda t: finish_softmax(), 1)
        during(14, attend_chunk)

    for t in range(1, SEQ_DEVICES):
        remote(oa_s.at[t], ob.at[behind(t)], oa_ss.at[t], oa_rs.at[t], (ahead(t), res)).wait_recv()

    @pl.loop(0, 8)
    def _(pair):
        flipped = []
        for k in range(2):
            s = pair * 2 + k
            rows = pl.ds(pl.multiple_of(s * 32, 32), 32)
            mixed = jnp.concatenate([ob[h, rows, :] for h in range(HEADS)], axis=0).astype(F32)
            flipped.append((gates[s] * mixed).astype(BF16).astype(F32).T.astype(BF16))
        update = jnp.concatenate(flipped, axis=0)
        rows = pl.ds(pl.multiple_of(pair * 256, 256), 256)
        total = x[rows, :].astype(F32) + matmul(update, wf[...])
        total = total.astype(BF16)
        for k in range(2):
            after[pair * 2 + k] = total[128 * k : 128 * k + 128, :]

    def columns(t):
        g = ahead(t)
        return remote(
            after.at[:, pl.ds(pl.multiple_of(g * 16, 16), 16), :],
            out.at[pl.ds(pl.multiple_of(me * 16, 16), 16)],
            col_s.at[t], col_r.at[t], (g, res),
        )

    mine = pl.ds(pl.multiple_of(me * 16, 16), 16)
    own_c = pltpu.make_async_copy(after.at[:, mine, :], out.at[mine], own_s.at[3])
    own_c.start()
    for t in range(1, SEQ_DEVICES):
        columns(t).start()
    own_c.wait()
    for t in range(1, SEQ_DEVICES):
        columns(t).wait_send()
        remote(
            after.at[:, mine, :],
            out.at[pl.ds(pl.multiple_of(behind(t) * 16, 16), 16)],
            col_s.at[t], col_r.at[t], (ahead(t), res),
        ).wait_recv()

    stat_copy(0, twin).wait_send()
    stat_copy(1, beside).wait_send()
    stat_copy(2, across).wait_send()

    @pl.loop(0, 8)
    def _(t):
        @pl.when(t > 0)
        def _():
            ka(t).wait_send()
            qa(t).wait_send()
            va(t).wait_send()
            oa(t).wait_send()

        for buf in (kzs, vzs):
            for copy in ring(*buf, t):
                copy.wait_send()

            @pl.when(lax.rem(t, 2) == 0)
            def _():
                onward_up(*buf, t).wait_send()

            @pl.when(lax.rem(t, 2) == 1)
            def _():
                onward_down(*buf, t).wait_send()

        q_twin(t).wait_send()
        q_beside(t).wait_send()
        q_onward(t).wait_send()
        oc(t).wait_send()
        oy(t).wait_send()


def row_attention(x, wq, wk, wv, wg, wf):
    dma = pltpu.SemaphoreType.DMA
    vmem = pltpu.VMEM
    return pl.pallas_call(
        row_kernel,
        name="row_attention",
        out_shape=jax.ShapeDtypeStruct((128, 16, 256), BF16),
        in_specs=[pl.BlockSpec(memory_space=vmem)] * 6,
        out_specs=pl.BlockSpec(memory_space=vmem),
        scratch_shapes=[
            vmem((2048, 256), BF16),
            vmem((1024, 256), BF16),
            vmem((8, 128, 512), BF16),
            vmem((8, 512, 128), BF16),
            vmem((8, 512, 128), BF16),
            vmem((4, 8, 128, 512), BF16),
            vmem((4, 8, 512, 128), BF16),
            vmem((4, 8, 512, 128), BF16),
            vmem((512, 512), F32),
            vmem((512, 512), BF16),
            vmem((16, 256, 128), F32),
            vmem((4, 2, 8, 512), F32),
            vmem((2, 4, 512, 128), F32),
            vmem((8, 2, 512, 128), BF16),
            vmem((8, 2, 512, 128), BF16),
            vmem((8, 512, 128), BF16),
            vmem((8, 512, 128), BF16),
            vmem((8, 512, 128), BF16),
            vmem((8, 512, 128), BF16),
            vmem((16, 128, 256), BF16),
        ]
        + [dma((8,))] * 6
        + [dma((3, 8))] * 6
        + [dma((3,))] * 2
        + [dma((8,))] * 8
        + [dma((4,))],
        compiler_params=pltpu.CompilerParams(
            collective_id=0, has_side_effects=True, vmem_limit_bytes=60 * 2**20
        ),
    )(x, wq, wk, wv, wg, wf)


def swap_matrix():
    a = lax.broadcasted_iota(jnp.int32, (256, 256), 0)
    b = lax.broadcasted_iota(jnp.int32, (256, 256), 1)
    return jnp.where(b == ((a & 15) << 4) + (a >> 4), 1.0, 0.0).astype(BF16)


def column_kernel(
    xc, wq, wk, wv, wg, wf, we, ws, out,
    swap, x2, wt, wide, done, back, send_sem, recv_sem,
):
    me = lax.axis_index("seq")
    res = lax.axis_index("res")

    def ahead(t):
        return lax.rem(me + t, SEQ_DEVICES)

    def behind(t):
        return lax.rem(me + SEQ_DEVICES - t, SEQ_DEVICES)

    barrier = pltpu.get_barrier_semaphore()
    for t in range(1, SEQ_DEVICES):
        pl.semaphore_signal(barrier, inc=1, device_id=(ahead(t), res), device_id_type=MESH)

    swap[...] = swap_matrix()
    wt[0:256, :] = flip(wq[...])
    wt[256:512, :] = flip(wv[...])
    wt[512:768, :] = flip(wg[...])
    wide[...] = jnp.zeros_like(wide)

    @pl.loop(0, 8)
    def _(g):
        rows = pl.ds(pl.multiple_of(g * 256, 256), 256)
        turned = matmul(swap[...], xc[rows, :]).astype(BF16)
        for r in range(16):
            x2[pl.ds(pl.multiple_of(r * 128 + g * 16, 16), 16), :] = turned[16 * r : 16 * r + 16, :]

    pl.semaphore_wait(barrier, SEQ_DEVICES - 1)
    scale = 1.0 / math.sqrt(HEAD_DIM)

    def result(block, t):
        g = ahead(t)
        return remote(
            done.at[pl.ds(block * 4, 4), pl.ds(pl.multiple_of(g * 16, 16), 16), :],
            back.at[pl.ds(me * 16 + block * 4, 4)],
            send_sem.at[block, t], recv_sem.at[block, t], (g, res),
        )

    @pl.loop(0, 4)
    def _(block):
        rows = pl.ds(pl.multiple_of(block * 512, 512), 512)
        entries = x2[rows, :].astype(F32)
        part = layer_normalize(entries).astype(BF16)
        keys = matmul(part, wk[...]).astype(BF16)
        turned = matmul_nt(wt[...], part)
        queries = turned[0:256, :].astype(BF16)
        values = turned[256:512, :].astype(BF16)
        gate = jax.nn.sigmoid(turned[512:768, :])
        updates = []
        for r in range(4):
            lanes = slice(128 * r, 128 * r + 128)
            for h in range(HEADS):
                wide[r, 32 * h : 32 * h + 32, 128 * h : 128 * h + 128] = queries[
                    32 * h : 32 * h + 32, lanes
                ]
            scores = matmul(keys[lanes, :], wide[r])
            highest = jnp.max(scores, axis=0, keepdims=True)
            expo = jnp.exp((scores - highest) * scale)
            total = jnp.sum(expo, axis=0, keepdims=True)
            weights = (expo * (1.0 / total)).astype(BF16)
            mixed = []
            for h in range(0, HEADS, 2):
                both = matmul(values[32 * h : 32 * h + 64, lanes], weights[:, 128 * h : 128 * h + 256])
                mixed += [both[0:32, 0:128], both[32:64, 128:256]]
            mixed = jnp.concatenate(mixed, axis=0)
            updates.append((gate[:, lanes] * mixed).astype(BF16).astype(F32).T.astype(BF16))
        update = jnp.concatenate(updates, axis=0)
        after = (entries + matmul(update, wf[...])).astype(BF16).astype(F32)
        hidden = matmul(layer_normalize(after).astype(BF16), we[...])
        hidden = jnp.maximum(hidden, 0.0).astype(BF16)
        total = (after + matmul(hidden, ws[...])).astype(BF16)
        for r in range(4):
            done[block * 4 + r] = total[128 * r : 128 * r + 128, :]
        for t in range(1, SEQ_DEVICES):
            result(block, t).start()

    def finish(g, blocks):
        turned = matmul(swap[...], blocks).astype(BF16)
        for s in range(16):
            out[s, pl.ds(pl.multiple_of(g * 16, 16), 16), :] = turned[16 * s : 16 * s + 16, :]

    mine = done[:, pl.ds(pl.multiple_of(me * 16, 16), 16), :]
    finish(me, mine.reshape(256, 256))

    @pl.loop(1, 8)
    def _(t):
        g = behind(t)
        for block in range(4):
            remote(
                done.at[pl.ds(0, 4), pl.ds(0, 16), :],
                back.at[pl.ds(g * 16 + block * 4, 4)],
                send_sem.at[block, t], recv_sem.at[block, t], (ahead(t), res),
            ).wait_recv()
        finish(g, back[pl.ds(g * 16, 16)].reshape(256, 256))

    @pl.loop(1, 8)
    def _(t):
        for block in range(4):
            result(block, t).wait_send()


def column_attention(xc, wq, wk, wv, wg, wf, we, ws):
    vmem = pltpu.VMEM
    return pl.pallas_call(
        column_kernel,
        name="column_attention",
        out_shape=jax.ShapeDtypeStruct((16, 128, 256), BF16),
        in_specs=[pl.BlockSpec(memory_space=vmem)] * 8,
        out_specs=pl.BlockSpec(memory_space=vmem),
        scratch_shapes=[
            vmem((256, 256), BF16),
            vmem((2048, 256), BF16),
            vmem((768, 256), BF16),
            vmem((4, 256, 1024), BF16),
            vmem((16, 128, 256), BF16),
            vmem((128, 16, 256), BF16),
            pltpu.SemaphoreType.DMA((4, 8)),
            pltpu.SemaphoreType.DMA((4, 8)),
        ],
        compiler_params=pltpu.CompilerParams(
            collective_id=1, has_side_effects=True, vmem_limit_bytes=60 * 2**20
        ),
    )(xc, wq, wk, wv, wg, wf, we, ws)


def on_device(
    homolog_tensor,
    horizontal_probe_matrix,
    horizontal_lookup_matrix,
    horizontal_payload_matrix,
    horizontal_sigmoid_matrix,
    horizontal_final_matrix,
    vertical_probe_matrix,
    vertical_lookup_matrix,
    vertical_payload_matrix,
    vertical_sigmoid_matrix,
    vertical_final_matrix,
    expanding_matrix,
    shrinking_matrix,
):
    columns = row_attention(
        homolog_tensor.reshape(2048, 256),
        horizontal_probe_matrix,
        horizontal_lookup_matrix,
        horizontal_payload_matrix,
        horizontal_sigmoid_matrix,
        horizontal_final_matrix,
    )
    return column_attention(
        columns.reshape(2048, 256),
        vertical_probe_matrix,
        vertical_lookup_matrix,
        vertical_payload_matrix,
        vertical_sigmoid_matrix,
        vertical_final_matrix,
        expanding_matrix,
        shrinking_matrix,
    )


def solution(mesh):
    in_specs = (P("seq", "res", None), P(), P(), P(), P(), P(), P(), P(), P(), P(), P(), P(), P())
    out_specs = P("seq", "res", None)
    return jax.shard_map(
        on_device, mesh=mesh, in_specs=in_specs, out_specs=out_specs, check_vma=False
    )
```

```python
import math

import jax
import jax.numpy as jnp
from jax import lax
from jax.experimental import pallas as pl
from jax.experimental.pallas import tpu as pltpu
from jax.sharding import PartitionSpec as P

HEADS = 8
HEAD_DIM = 32
SEQ_DEVICES = 8
MESH = pl.DeviceIdType.MESH
BF16 = jnp.bfloat16
F32 = jnp.float32
NT = (((1,), (1,)), ((), ()))


def layer_normalize(entries):
    center = entries - jnp.mean(entries, axis=-1, keepdims=True)
    spread = jnp.mean(center * center, axis=-1, keepdims=True)
    return center * lax.rsqrt(spread + 1e-05)


def matmul(a, b):
    return jnp.dot(a, b, preferred_element_type=F32)


def matmul_nt(a, b):
    return lax.dot_general(a, b, NT, preferred_element_type=F32)


def flip(a):
    return a.astype(F32).T.astype(BF16)


def remote(src, dst, send, recv, device):
    return pltpu.make_async_remote_copy(
        src_ref=src, dst_ref=dst, send_sem=send, recv_sem=recv, device_id=device, device_id_type=MESH
    )


class Exchange:
    def __init__(self, place, src, dst, mid, slot, send, recv, onward_device):
        self.yh, self.xx, self.me, self.res = place
        self.src, self.dst, self.mid, self.slot = src, dst, mid, slot
        self.send, self.recv = send, recv
        self.onward_device = onward_device

    def near(self, k):
        to = self.yh * 4 + lax.rem(self.xx + 4 - k, 4)
        return remote(
            self.src.at[to], self.dst.at[self.slot, self.me],
            self.send.at[0, k], self.recv.at[0, k], (to, self.res),
        )

    def far(self, k):
        column = lax.rem(self.xx + 4 - k, 4)
        return remote(
            self.src.at[(1 - self.yh) * 4 + column], self.mid.at[k],
            self.send.at[1, k], self.recv.at[1, k], (self.yh * 4 + column, self.res),
        )

    def onward(self, k):
        origin = self.yh * 4 + lax.rem(self.xx + k, 4)
        src = self.src.at[(1 - self.yh) * 4 + self.xx] if k == 0 else self.mid.at[k]
        return remote(
            src, self.dst.at[self.slot, origin],
            self.send.at[2, k], self.recv.at[2, k], self.onward_device,
        )

    def start(self):
        for k in (1, 3, 2):
            self.far(k).start()
            self.near(k).start()
        self.onward(0).start()

    def forward(self, k):
        for i in range(1, 4):

            @pl.when(k == i)
            def _(i=i):
                self.far(i).wait_recv()
                self.onward(i).start()

    def arrived(self, place, t):
        @pl.when(t < 4)
        def _():
            remote(
                place, place, self.send.at[0, t], self.recv.at[0, t], self.onward_device
            ).wait_recv()

        @pl.when(t >= 4)
        def _():
            remote(
                place, place, self.send.at[2, t - 4], self.recv.at[2, t - 4], self.onward_device
            ).wait_recv()

    def drain(self):
        for k in range(1, 4):
            self.near(k).wait_send()
            self.far(k).wait_send()
        for k in range(4):
            self.onward(k).wait_send()


def swap_matrix():
    a = lax.broadcasted_iota(jnp.int32, (256, 256), 0)
    b = lax.broadcasted_iota(jnp.int32, (256, 256), 1)
    return jnp.where(b == ((a & 15) << 4) + (a >> 4), 1.0, 0.0).astype(BF16)


def pick_matrix(block, quarter):
    k = lax.broadcasted_iota(jnp.int32, (256, 256), 0) + block * 256
    n = lax.broadcasted_iota(jnp.int32, (256, 256), 1)
    same = ((k >> 7) == (n >> 5)) & (((k >> 5) & 3) == quarter) & ((k & 31) == (n & 31))
    return jnp.where(same, 1.0, 0.0).astype(BF16)


def kernel(
    x, wq, wk, wv, wg, wf, cq, ck, cv, cg, cf, ce, cs, out,
    normed, wt, ks, qs, vs, kmid, qmid, vmid, kz, vz, qg, logits, probs, stats,
    o_part, oc_s, oc_r, oy_s, oy_r, oa_s, oh, xc, gates, picks, osc,
    swap, x2, wide, done, back,
    ka_s, ka_r, qa_s, qa_r, va_s, va_r, kz_s, kz_r, vz_s, vz_r, qp_s, qp_r,
    st_s, st_r, oc_ss, oc_rs, oy_ss, oy_rs, oa_ss, oa_rs, col_s, col_r, back_s, back_r, own_s,
):
    me = lax.axis_index("seq")
    res = lax.axis_index("res")
    z = res // 4
    yl = lax.rem(res // 2, 2)
    c = lax.rem(res, 2)
    here = lax.rem(res, 4)
    yh = me // 4
    xx = lax.rem(me, 4)

    def at_res(zz, yy, cc):
        return (me, zz * 4 + yy * 2 + cc)

    z_up = lax.rem(z + 1, 4)
    z_down = lax.rem(z + 3, 4)
    z_far = lax.rem(z + 2, 4)
    up = at_res(z_up, yl, c)
    down = at_res(z_down, yl, c)
    twin = at_res(z, yl, 1 - c)
    beside = at_res(z, 1 - yl, c)
    across = at_res(z, 1 - yl, 1 - c)
    res_beside = z * 4 + (1 - yl) * 2 + c
    opposite = ((1 - yh) * 4 + xx, res)
    here_twin = yl * 2 + (1 - c)
    here_beside = (1 - yl) * 2 + c
    here_across = (1 - yl) * 2 + (1 - c)

    def diagonal(k):
        return ((1 - yh) * 4 + lax.rem(xx + 4 - k, 4), res_beside)

    def ahead(t):
        return lax.rem(yh + t // 4, 2) * 4 + lax.rem(xx + lax.rem(t, 4), 4)

    def turn(t):
        return lax.rem(me + t, SEQ_DEVICES)

    def unturn(t):
        return lax.rem(me + SEQ_DEVICES - t, SEQ_DEVICES)

    barrier = pltpu.get_barrier_semaphore()
    partners = [(turn(t), res) for t in range(1, SEQ_DEVICES)] + [up, down, twin, beside, across]
    partners += [diagonal(k) for k in range(4)]
    for device in partners:
        pl.semaphore_signal(barrier, inc=1, device_id=device, device_id_type=MESH)

    wt[0:256, :] = flip(wk[...])

    @pl.loop(0, 4)
    def _(quad):
        rows = pl.ds(pl.multiple_of(quad * 512, 512), 512)
        entries = x[pl.ds(quad * 4, 4)].reshape(512, 256)
        part = layer_normalize(entries.astype(F32)).astype(BF16)
        normed[rows, :] = part
        keys = matmul_nt(wt[0:256, :], part).astype(BF16)
        for h in range(HEADS):
            for s in range(4):
                place = pl.ds(pl.multiple_of(quad * 128 + 32 * s, 32), 32)
                ks[h, place, :] = keys[32 * h : 32 * h + 32, 128 * s : 128 * s + 128]

    pl.semaphore_wait(barrier, len(partners))

    place = (yh, xx, me, res)
    ka = Exchange(place, ks, kz, kmid, z, ka_s, ka_r, opposite)
    va = Exchange(place, vs, vz, vmid, z, va_s, va_r, opposite)
    qa = Exchange(place, qs, qg, qmid, here, qa_s, qa_r, diagonal(0))

    own_k = pltpu.make_async_copy(ks.at[me], kz.at[z, me], own_s.at[0])
    own_q = pltpu.make_async_copy(qs.at[me], qg.at[here, me], own_s.at[1])
    own_v = pltpu.make_async_copy(vs.at[me], vz.at[z, me], own_s.at[2])
    own_k.start()
    ka.start()

    wt[256:512, :] = flip(wq[...])
    wt[512:768, :] = flip(wv[...])

    def project(quad, first, target):
        rows = pl.ds(pl.multiple_of(quad * 512, 512), 512)
        turned = matmul_nt(wt[first : first + 256, :], normed[rows, :])
        lanes = pl.ds(pl.multiple_of(quad * 128, 128), 128)
        for h in range(HEADS):
            block = turned[32 * h : 32 * h + 32, :]
            stack = jnp.concatenate([block[:, 128 * s : 128 * s + 128] for s in range(4)], axis=0)
            target[h, :, lanes] = stack.T.astype(BF16)

    def ring(buf, send, recv, t):
        g = ahead(t)
        return (
            remote(buf.at[z, g], buf.at[z, g], send.at[0, t], recv.at[0, t], up),
            remote(buf.at[z, g], buf.at[z, g], send.at[1, t], recv.at[1, t], down),
        )

    def ring_arrived(buf, send, recv, t):
        g = ahead(t)
        remote(buf.at[z_down, g], buf.at[z_down, g], send.at[0, t], recv.at[0, t], up).wait_recv()
        remote(buf.at[z_up, g], buf.at[z_up, g], send.at[1, t], recv.at[1, t], down).wait_recv()

    def onward_up(buf, send, recv, t):
        g = ahead(t)
        return remote(buf.at[z_down, g], buf.at[z_down, g], send.at[2, t], recv.at[2, t], up)

    def onward_down(buf, send, recv, t):
        g = ahead(t)
        return remote(buf.at[z_up, g], buf.at[z_up, g], send.at[2, t], recv.at[2, t], down)

    def far_arrived(buf, send, recv, t):
        g = ahead(t)
        remote(buf.at[z_far, g], buf.at[z_far, g], send.at[2, t], recv.at[2, t], up).wait_recv()

    def ring_forward(buf, send, recv, t):
        ring_arrived(buf, send, recv, t)

        @pl.when(lax.rem(t, 2) == 0)
        def _():
            onward_up(buf, send, recv, t).start()

        @pl.when(lax.rem(t, 2) == 1)
        def _():
            onward_down(buf, send, recv, t).start()

    kzs = (kz, kz_s, kz_r)
    vzs = (vz, vz_s, vz_r)

    def first_place(t):
        half = t // 4
        return here * (1 - half) + here_beside * half

    def second_place(t):
        half = t // 4
        return here_beside * (1 - half) + here * half

    def q_twin(t):
        spot = qg.at[first_place(t), ahead(t)]
        return remote(spot, spot, qp_s.at[0, t], qp_r.at[0, t], twin)

    def q_beside(t):
        spot = qg.at[first_place(t), ahead(t)]
        return remote(spot, spot, qp_s.at[1, t], qp_r.at[1, t], beside)

    def q_onward(t):
        spot = qg.at[second_place(t), ahead(t)]
        return remote(spot, spot, qp_s.at[2, t], qp_r.at[2, t], twin)

    def q_peers(t):
        @pl.when(t == 0)
        def _():
            own_q.wait()

        @pl.when(t > 0)
        def _():
            qa.arrived(qg.at[first_place(t), ahead(t)], t)

        q_beside(t).start()
        q_twin(t).start()

    def q_forward(t):
        spot = qg.at[second_place(t), ahead(t)]
        remote(spot, spot, qp_s.at[1, t], qp_r.at[1, t], beside).wait_recv()
        q_onward(t).start()

    def q_arrived(t):
        half = t // 4
        spot = qg.at[here_twin * (1 - half) + here_across * half, ahead(t)]
        remote(spot, spot, qp_s.at[0, t], qp_r.at[0, t], twin).wait_recv()
        spot = qg.at[here_across * (1 - half) + here_twin * half, ahead(t)]
        remote(spot, spot, qp_s.at[2, t], qp_r.at[2, t], twin).wait_recv()

    def add_chunk(t):
        far_arrived(*kzs, t)
        q_arrived(t)
        g = ahead(t)
        keys = jnp.concatenate([kz[zz, g] for zz in range(4)], axis=1)
        for p in range(4):
            rows = slice(128 * p, 128 * p + 128)
            term = matmul(qg[p, g], keys)

            @pl.when(t == 0)
            def _():
                logits[rows, :] = term

            @pl.when(t > 0)
            def _():
                logits[rows, :] += term

    scale = 1.0 / math.sqrt(SEQ_DEVICES * 16 * HEAD_DIM)

    def stat_copy(i, device):
        return remote(stats.at[here], stats.at[here], st_s.at[i], st_r.at[i], device)

    def stat_wait(i, spot):
        remote(stats.at[spot], stats.at[spot], st_s.at[i], st_r.at[i], twin).wait_recv()

    def local_softmax():
        for p in range(4):
            rows = slice(128 * p, 128 * p + 128)
            highest = jnp.max(logits[rows, :], axis=1, keepdims=True)
            expo = jnp.exp((logits[rows, :] - highest) * scale)
            logits[rows, :] = expo
            total = jnp.sum(expo, axis=1, keepdims=True)
            stats[here, 0, :, rows] = jnp.broadcast_to(highest, (128, 128)).T[0:8, :]
            stats[here, 1, :, rows] = jnp.broadcast_to(total, (128, 128)).T[0:8, :]
        stat_copy(1, beside).start()
        stat_copy(2, across).start()
        stat_copy(0, twin).start()

    def finish_softmax():
        stat_wait(0, here_twin)
        stat_wait(1, here_beside)
        stat_wait(2, here_across)
        highest = stats[0, 0]
        for p in range(1, 4):
            highest = jnp.maximum(highest, stats[p, 0])
        total = jnp.zeros((8, 512), F32)
        for p in range(4):
            total += stats[p, 1] * jnp.exp((stats[p, 0] - highest) * scale)
        factor = jnp.exp((stats[here, 0] - highest) * scale) / total
        for p in range(4):
            rows = slice(128 * p, 128 * p + 128)
            column = jnp.broadcast_to(factor[0:1, rows], (128, 128)).T
            for q in range(4):
                lanes = slice(128 * q, 128 * q + 128)
                probs[rows, lanes] = (logits[rows, lanes] * column).astype(BF16)

    def oc(t):
        return remote(oc_s.at[t], oc_r.at[t], oc_ss.at[t], oc_rs.at[t], twin)

    def oy(t):
        return remote(oy_s.at[t], oy_r.at[t], oy_ss.at[t], oy_rs.at[t], beside)

    def attend(t):
        far_arrived(*vzs, t)
        g = ahead(t)
        slot = lax.rem(t, 2)
        values = jnp.concatenate([vz[zz, g] for zz in range(4)], axis=0)
        for p in range(4):
            o_part[slot, p] = matmul(probs[128 * p : 128 * p + 128, :], values)
        for y in range(2):
            oc_s[t, y] = o_part[slot, 2 * y + 1 - c].astype(BF16)
        oc(t).start()

    same = pl.ds(pl.multiple_of(yh * 64, 64), 64)
    other = pl.ds(pl.multiple_of((1 - yh) * 64, 64), 64)

    def add_twin(t):
        slot = lax.rem(t, 2)
        oc(t).wait_recv()
        oy_s[t, 0] = (o_part[slot, here, other, :] + oc_r[t, yl, other, :].astype(F32)).astype(BF16)
        oy_s[t, 1] = (o_part[slot, here_beside, same, :] + oc_r[t, 1 - yl, same, :].astype(F32)).astype(BF16)
        oy(t).start()

    def oa_near(t, k):
        column = lax.rem(xx + 4 - k, 4)
        return remote(
            oa_s.at[t, 0, pl.ds(pl.multiple_of(column * 16, 16), 16), :], oh.at[me, ahead(t)],
            oa_ss.at[t, k], oa_rs.at[t, k], (yh * 4 + column, res),
        )

    def oa_far(t, k):
        column = lax.rem(xx + 4 - k, 4)
        return remote(
            oa_s.at[t, 1, pl.ds(pl.multiple_of(column * 16, 16), 16), :], oh.at[me, ahead(t)],
            oa_ss.at[t, 4 + k], oa_rs.at[t, 4 + k], diagonal(k),
        )

    def oa_wait(t, k):
        for far in (0, 1):
            if k == 0 and far == 0:
                continue
            yhs = lax.rem(yh + far, 2)
            xs = lax.rem(xx + k, 4)
            g = lax.rem(yhs + t // 4, 2) * 4 + lax.rem(xs + lax.rem(t, 4), 4)
            spot = oh.at[yhs * 4 + xs, g]
            remote(spot, spot, oa_ss.at[t, 4 * far + k], oa_rs.at[t, 4 * far + k], beside).wait_recv()

    def add_beside(t):
        slot = lax.rem(t, 2)
        oy(t).wait_recv()
        oa_s[t, 1] = (
            o_part[slot, here_beside, other, :]
            + oc_r[t, 1 - yl, other, :].astype(F32)
            + oy_r[t, 0].astype(F32)
        ).astype(BF16)
        for k in (2, 1, 3, 0):
            oa_far(t, k).start()
        oa_s[t, 0] = (
            o_part[slot, here, same, :]
            + oc_r[t, yl, same, :].astype(F32)
            + oy_r[t, 1].astype(F32)
        ).astype(BF16)
        for k in (2, 1, 3):
            oa_near(t, k).start()
        oh[me, ahead(t)] = oa_s[t, 0, pl.ds(pl.multiple_of(xx * 16, 16), 16), :]

    mine = pl.ds(pl.multiple_of(me * 16, 16), 16)
    own_x = pltpu.make_async_copy(x.at[:, mine, :], xc.at[mine], own_s.at[3])

    def x_copy(t):
        g = turn(t)
        return remote(
            x.at[:, pl.ds(pl.multiple_of(g * 16, 16), 16), :], xc.at[mine],
            col_s.at[t], col_r.at[t], (g, res),
        )

    def x_start():
        own_x.start()
        for t in range(1, SEQ_DEVICES):
            x_copy(t).start()

    def x_arrived():
        own_x.wait()
        for t in range(1, SEQ_DEVICES):
            spot = xc.at[pl.ds(pl.multiple_of(unturn(t) * 16, 16), 16)]
            remote(spot, spot, col_s.at[t], col_r.at[t], (turn(t), res)).wait_recv()

    def gate_block(i):
        rows = pl.ds(pl.multiple_of(i * 512, 512), 512)
        entries = xc[pl.ds(pl.multiple_of(i * 32, 32), 32)].reshape(512, 256).astype(F32)
        gates[rows, :] = jax.nn.sigmoid(matmul(layer_normalize(entries).astype(BF16), wg[...]))

    def prepare(i):
        @pl.when(i == 0)
        def _():
            wt[0:256, :] = flip(cq[...])
            swap[...] = swap_matrix()

        @pl.when(i == 1)
        def _():
            wt[256:512, :] = flip(cv[...])
            wt[512:768, :] = flip(cg[...])

        for quarter in range(4):
            picks[quarter, pl.ds(pl.multiple_of(i * 256, 256), 256), :] = pick_matrix(i, quarter)
        wide[i] = jnp.zeros((256, 1024), BF16)

    @pl.loop(0, 4)
    def _(quad):
        project(quad, 256, qs)

    own_q.start()
    qa.start()

    def v_project(t):
        project(t, 512, vs)

        @pl.when(t == 3)
        def _():
            own_v.start()
            va.start()

    def k_own(t):
        @pl.when(t == 0)
        def _():
            own_k.wait()

        @pl.when(t > 0)
        def _():
            ka.arrived(kz.at[z, ahead(t)], t)

        for copy in ring(*kzs, t):
            copy.start()

    def v_own(t):
        @pl.when(t == 0)
        def _():
            own_v.wait()

        @pl.when(t > 0)
        def _():
            va.arrived(vz.at[z, ahead(t)], t)

        for copy in ring(*vzs, t):
            copy.start()

    @pl.loop(0, 23)
    def _(tick):
        def during(first, action, count=8):
            @pl.when((tick >= first) & (tick < first + count))
            def _():
                action(tick - first)

        during(15, add_beside)
        during(14, add_twin)
        during(0, k_own)
        during(0, lambda t: ka.forward(t + 1), 3)
        during(0, v_project, 4)
        during(8, v_own)
        during(2, lambda t: ring_forward(*kzs, t))
        during(10, lambda t: ring_forward(*vzs, t))
        during(2, lambda t: qa.forward(t + 1), 3)
        during(5, lambda t: va.forward(t + 1), 3)
        during(2, q_peers)
        during(3, q_forward)
        during(4, prepare, 4)
        during(8, lambda t: x_start(), 1)
        during(4, add_chunk)
        during(12, lambda t: local_softmax(), 1)
        during(13, lambda t: finish_softmax(), 1)
        during(13, attend)
        during(14, lambda t: x_arrived(), 1)
        during(14, gate_block, 4)

    @pl.loop(0, 8)
    def _(t):
        for k in range(4):
            oa_wait(t, k)

    @pl.loop(0, 4)
    def _(quarter):
        stack = jnp.concatenate(
            [
                jnp.concatenate(
                    [oh[h, :, :, 128 * q : 128 * q + 128].reshape(128, 128) for h in range(HEADS)], axis=1
                )
                for q in range(4)
            ],
            axis=0,
        )
        spread = matmul(stack, picks[quarter]).astype(BF16)
        for q in range(4):
            osc[:, 4 * q + quarter] = spread[128 * q : 128 * q + 128, :].reshape(8, 16, 256)

    @pl.loop(0, 8)
    def _(g):
        rows = pl.ds(pl.multiple_of(g * 256, 256), 256)
        update = (gates[rows, :] * osc[g].reshape(256, 256).astype(F32)).astype(BF16)
        entries = xc[pl.ds(pl.multiple_of(g * 16, 16), 16)].reshape(256, 256).astype(F32)
        after = (entries + matmul(update, wf[...])).astype(BF16)
        turned = matmul(swap[...], after).astype(BF16)
        for r in range(16):
            x2[pl.ds(pl.multiple_of(r * 128 + g * 16, 16), 16), :] = turned[16 * r : 16 * r + 16, :]

    col_scale = 1.0 / math.sqrt(HEAD_DIM)

    def result(block, t):
        g = turn(t)
        return remote(
            done.at[pl.ds(block * 4, 4), pl.ds(pl.multiple_of(g * 16, 16), 16), :],
            back.at[pl.ds(me * 16 + block * 4, 4)],
            back_s.at[block, t], back_r.at[block, t], (g, res),
        )

    @pl.loop(0, 4)
    def _(block):
        rows = pl.ds(pl.multiple_of(block * 512, 512), 512)
        entries = x2[rows, :].astype(F32)
        part = layer_normalize(entries).astype(BF16)
        keys = matmul(part, ck[...]).astype(BF16)
        turned = matmul_nt(wt[...], part)
        queries = turned[0:256, :].astype(BF16)
        values = turned[256:512, :].astype(BF16)
        gate = jax.nn.sigmoid(turned[512:768, :])
        updates = []
        for r in range(4):
            lanes = slice(128 * r, 128 * r + 128)
            for h in range(HEADS):
                wide[r, 32 * h : 32 * h + 32, 128 * h : 128 * h + 128] = queries[
                    32 * h : 32 * h + 32, lanes
                ]
            scores = matmul(keys[lanes, :], wide[r])
            highest = jnp.max(scores, axis=0, keepdims=True)
            expo = jnp.exp((scores - highest) * col_scale)
            total = jnp.sum(expo, axis=0, keepdims=True)
            weights = (expo * (1.0 / total)).astype(BF16)
            mixed = []
            for h in range(0, HEADS, 2):
                both = matmul(values[32 * h : 32 * h + 64, lanes], weights[:, 128 * h : 128 * h + 256])
                mixed += [both[0:32, 0:128], both[32:64, 128:256]]
            mixed = jnp.concatenate(mixed, axis=0)
            updates.append((gate[:, lanes] * mixed).astype(BF16).astype(F32).T.astype(BF16))
        update = jnp.concatenate(updates, axis=0)
        after = (entries + matmul(update, cf[...])).astype(BF16).astype(F32)
        hidden = matmul(layer_normalize(after).astype(BF16), ce[...])
        hidden = jnp.maximum(hidden, 0.0).astype(BF16)
        total = (after + matmul(hidden, cs[...])).astype(BF16)
        for r in range(4):
            done[block * 4 + r] = total[128 * r : 128 * r + 128, :]
        for t in range(1, SEQ_DEVICES):
            result(block, t).start()

    def finish(g, blocks):
        turned = matmul(swap[...], blocks).astype(BF16)
        for s in range(16):
            out[s, pl.ds(pl.multiple_of(g * 16, 16), 16), :] = turned[16 * s : 16 * s + 16, :]

    finish(me, done[:, mine, :].reshape(256, 256))

    @pl.loop(1, 8)
    def _(t):
        g = unturn(t)
        for block in range(4):
            spot = back.at[pl.ds(g * 16 + block * 4, 4)]
            remote(spot, spot, back_s.at[block, t], back_r.at[block, t], (turn(t), res)).wait_recv()
        finish(g, back[pl.ds(g * 16, 16)].reshape(256, 256))

    for exchange in (ka, qa, va):
        exchange.drain()
    stat_copy(0, twin).wait_send()
    stat_copy(1, beside).wait_send()
    stat_copy(2, across).wait_send()

    @pl.loop(0, 8)
    def _(t):
        for buf in (kzs, vzs):
            for copy in ring(*buf, t):
                copy.wait_send()

            @pl.when(lax.rem(t, 2) == 0)
            def _():
                onward_up(*buf, t).wait_send()

            @pl.when(lax.rem(t, 2) == 1)
            def _():
                onward_down(*buf, t).wait_send()

        q_twin(t).wait_send()
        q_beside(t).wait_send()
        q_onward(t).wait_send()
        oc(t).wait_send()
        oy(t).wait_send()
        for k in range(4):
            oa_far(t, k).wait_send()
        for k in range(1, 4):
            oa_near(t, k).wait_send()

        @pl.when(t > 0)
        def _():
            x_copy(t).wait_send()
            for block in range(4):
                result(block, t).wait_send()


def on_device(
    homolog_tensor,
    horizontal_probe_matrix,
    horizontal_lookup_matrix,
    horizontal_payload_matrix,
    horizontal_sigmoid_matrix,
    horizontal_final_matrix,
    vertical_probe_matrix,
    vertical_lookup_matrix,
    vertical_payload_matrix,
    vertical_sigmoid_matrix,
    vertical_final_matrix,
    expanding_matrix,
    shrinking_matrix,
):
    dma = pltpu.SemaphoreType.DMA
    vmem = pltpu.VMEM
    return pl.pallas_call(
        kernel,
        name="msa_block",
        out_shape=jax.ShapeDtypeStruct((16, 128, 256), BF16),
        in_specs=[pl.BlockSpec(memory_space=vmem)] * 13,
        out_specs=pl.BlockSpec(memory_space=vmem),
        scratch_shapes=[
            vmem((2048, 256), BF16),
            vmem((768, 256), BF16),
            vmem((8, 512, 128), BF16),
            vmem((8, 128, 512), BF16),
            vmem((8, 128, 512), BF16),
            vmem((4, 512, 128), BF16),
            vmem((4, 128, 512), BF16),
            vmem((4, 128, 512), BF16),
            vmem((4, 8, 512, 128), BF16),
            vmem((4, 8, 128, 512), BF16),
            vmem((4, 8, 128, 512), BF16),
            vmem((512, 512), F32),
            vmem((512, 512), BF16),
            vmem((4, 2, 8, 512), F32),
            vmem((2, 4, 128, 512), F32),
            vmem((8, 2, 128, 512), BF16),
            vmem((8, 2, 128, 512), BF16),
            vmem((8, 2, 64, 512), BF16),
            vmem((8, 2, 64, 512), BF16),
            vmem((8, 2, 64, 512), BF16),
            vmem((8, 8, 16, 512), BF16),
            vmem((128, 16, 256), BF16),
            vmem((2048, 256), F32),
            vmem((4, 1024, 256), BF16),
            vmem((8, 16, 16, 256), BF16),
            vmem((256, 256), BF16),
            vmem((2048, 256), BF16),
            vmem((4, 256, 1024), BF16),
            vmem((16, 128, 256), BF16),
            vmem((128, 16, 256), BF16),
        ]
        + [dma((3, 4))] * 6
        + [dma((3, 8))] * 6
        + [dma((3,))] * 2
        + [dma((8,))] * 4
        + [dma((8, 8))] * 2
        + [dma((8,))] * 2
        + [dma((4, 8))] * 2
        + [dma((4,))],
        compiler_params=pltpu.CompilerParams(
            collective_id=0, has_side_effects=True, vmem_limit_bytes=62 * 2**20
        ),
    )(
        homolog_tensor,
        horizontal_probe_matrix,
        horizontal_lookup_matrix,
        horizontal_payload_matrix,
        horizontal_sigmoid_matrix,
        horizontal_final_matrix,
        vertical_probe_matrix,
        vertical_lookup_matrix,
        vertical_payload_matrix,
        vertical_sigmoid_matrix,
        vertical_final_matrix,
        expanding_matrix,
        shrinking_matrix,
    )


def solution(mesh):
    in_specs = (P("seq", "res", None), P(), P(), P(), P(), P(), P(), P(), P(), P(), P(), P(), P())
    out_specs = P("seq", "res", None)
    return jax.shard_map(
        on_device, mesh=mesh, in_specs=in_specs, out_specs=out_specs, check_vma=False
    )
```

```python
import math

import jax
import jax.numpy as jnp
from jax import lax
from jax.experimental import pallas as pl
from jax.experimental.pallas import tpu as pltpu
from jax.sharding import PartitionSpec as P

HEADS = 8
HEAD_DIM = 32
SEQ_DEVICES = 8
MESH = pl.DeviceIdType.MESH
BF16 = jnp.bfloat16
F32 = jnp.float32
NT = (((1,), (1,)), ((), ()))


def layer_normalize(entries):
    center = entries - jnp.mean(entries, axis=-1, keepdims=True)
    spread = jnp.mean(center * center, axis=-1, keepdims=True)
    return center * lax.rsqrt(spread + 1e-05)


def matmul(a, b):
    return jnp.dot(a, b, preferred_element_type=F32)


def matmul_nt(a, b):
    return lax.dot_general(a, b, NT, preferred_element_type=F32)


def flip(a):
    return a.astype(F32).T.astype(BF16)


def remote(src, dst, send, recv, device):
    return pltpu.make_async_remote_copy(
        src_ref=src, dst_ref=dst, send_sem=send, recv_sem=recv, device_id=device, device_id_type=MESH
    )


class Exchange:
    def __init__(self, place, src, dst, mid, slot, send, recv, onward_device):
        self.yh, self.xx, self.me, self.res = place
        self.src, self.dst, self.mid, self.slot = src, dst, mid, slot
        self.send, self.recv = send, recv
        self.onward_device = onward_device

    def near(self, k):
        to = self.yh * 4 + lax.rem(self.xx + 4 - k, 4)
        return remote(
            self.src.at[to], self.dst.at[self.slot, k],
            self.send.at[0, k], self.recv.at[0, k], (to, self.res),
        )

    def far(self, k):
        column = lax.rem(self.xx + 4 - k, 4)
        return remote(
            self.src.at[(1 - self.yh) * 4 + column], self.mid.at[k],
            self.send.at[1, k], self.recv.at[1, k], (self.yh * 4 + column, self.res),
        )

    def onward(self, k):
        src = self.src.at[(1 - self.yh) * 4 + self.xx] if k == 0 else self.mid.at[k]
        return remote(
            src, self.dst.at[self.slot, 4 + k],
            self.send.at[2, k], self.recv.at[2, k], self.onward_device,
        )

    def start(self):
        for k in (1, 3, 2):
            self.near(k).start()
        self.onward(0).start()
        for k in (1, 3, 2):
            self.far(k).start()

    def forward(self):
        for k in (1, 3, 2):
            self.far(k).wait_recv()
            self.onward(k).start()

    def arrived(self, place, pair, own):
        def wait(leg, k, t):
            spot = self.dst.at[place, t]
            remote(spot, spot, self.send.at[leg, k], self.recv.at[leg, k], self.onward_device).wait_recv()

        @pl.when(pair == 0)
        def _():
            own.wait()
            wait(0, 1, 1)

        @pl.when(pair == 1)
        def _():
            wait(0, 2, 2)
            wait(0, 3, 3)

        @pl.when(pair >= 2)
        def _():
            wait(2, 2 * pair - 4, 2 * pair)
            wait(2, 2 * pair - 3, 2 * pair + 1)

    def drain(self):
        for k in range(1, 4):
            self.near(k).wait_send()
            self.far(k).wait_send()
        for k in range(4):
            self.onward(k).wait_send()


def swap_matrix():
    a = lax.broadcasted_iota(jnp.int32, (256, 256), 0)
    b = lax.broadcasted_iota(jnp.int32, (256, 256), 1)
    return jnp.where(b == ((a & 15) << 4) + (a >> 4), 1.0, 0.0).astype(BF16)


def pick_matrix(block, quarter):
    k = lax.broadcasted_iota(jnp.int32, (256, 256), 0) + block * 256
    n = lax.broadcasted_iota(jnp.int32, (256, 256), 1)
    same = ((k >> 7) == (n >> 5)) & (((k >> 5) & 3) == quarter) & ((k & 31) == (n & 31))
    return jnp.where(same, 1.0, 0.0).astype(BF16)


def kernel(
    x, wq, wk, wv, wg, wf, cq, ck, cv, cg, cf, ce, cs, out,
    normed, wt, ks, qs, vs, kmid, qmid, vmid, kz, vz, qg, logits, probs, stats,
    o_part, oc_s, oc_r, oy_s, oy_r, oa_s, oh, xc, gates, picks, osc,
    swap, x2, wide, done,
    ka_s, ka_r, qa_s, qa_r, va_s, va_r, kz_s, kz_r, vz_s, vz_r, qp_s, qp_r,
    st_s, st_r, oc_ss, oc_rs, oy_ss, oy_rs, oa_ss, oa_rs, col_s, col_r, back_s, back_r, own_s,
):
    me = lax.axis_index("seq")
    res = lax.axis_index("res")
    z = res // 4
    yl = lax.rem(res // 2, 2)
    c = lax.rem(res, 2)
    here = lax.rem(res, 4)
    yh = me // 4
    xx = lax.rem(me, 4)

    def at_res(zz, yy, cc):
        return (me, zz * 4 + yy * 2 + cc)

    z_up = lax.rem(z + 1, 4)
    z_down = lax.rem(z + 3, 4)
    z_far = lax.rem(z + 2, 4)
    up = at_res(z_up, yl, c)
    down = at_res(z_down, yl, c)
    twin = at_res(z, yl, 1 - c)
    beside = at_res(z, 1 - yl, c)
    across = at_res(z, 1 - yl, 1 - c)
    res_beside = z * 4 + (1 - yl) * 2 + c
    opposite = ((1 - yh) * 4 + xx, res)
    here_twin = yl * 2 + (1 - c)
    here_beside = (1 - yl) * 2 + c
    here_across = (1 - yl) * 2 + (1 - c)

    def diagonal(k):
        return ((1 - yh) * 4 + lax.rem(xx + 4 - k, 4), res_beside)

    def pair_of(u):
        return pl.ds(u * 2, 2)

    def turn(t):
        return lax.rem(me + t, SEQ_DEVICES)

    def unturn(t):
        return lax.rem(me + SEQ_DEVICES - t, SEQ_DEVICES)

    barrier = pltpu.get_barrier_semaphore()
    partners = [(turn(t), res) for t in range(1, SEQ_DEVICES)] + [up, down, twin, beside, across]
    partners += [diagonal(k) for k in range(4)]
    for device in partners:
        pl.semaphore_signal(barrier, inc=1, device_id=device, device_id_type=MESH)

    wt[0:256, :] = flip(wk[...])

    @pl.loop(0, 4)
    def _(quad):
        rows = pl.ds(pl.multiple_of(quad * 512, 512), 512)
        entries = x[pl.ds(quad * 4, 4)].reshape(512, 256)
        part = layer_normalize(entries.astype(F32)).astype(BF16)
        normed[rows, :] = part
        keys = matmul_nt(wt[0:256, :], part).astype(BF16)
        for h in range(HEADS):
            for s in range(4):
                place = pl.ds(pl.multiple_of(quad * 128 + 32 * s, 32), 32)
                ks[h, place, :] = keys[32 * h : 32 * h + 32, 128 * s : 128 * s + 128]

    pl.semaphore_wait(barrier, len(partners))

    place = (yh, xx, me, res)
    ka = Exchange(place, ks, kz, kmid, z, ka_s, ka_r, opposite)
    va = Exchange(place, vs, vz, vmid, z, va_s, va_r, opposite)
    qa = Exchange(place, qs, qg, qmid, here, qa_s, qa_r, diagonal(0))

    own_k = pltpu.make_async_copy(ks.at[me], kz.at[z, 0], own_s.at[0])
    own_q = pltpu.make_async_copy(qs.at[me], qg.at[here, 0], own_s.at[1])
    own_v = pltpu.make_async_copy(vs.at[me], vz.at[z, 0], own_s.at[2])
    own_k.start()
    ka.start()

    wt[256:512, :] = flip(wq[...])
    wt[512:768, :] = flip(wv[...])

    def project(quad, first, target):
        rows = pl.ds(pl.multiple_of(quad * 512, 512), 512)
        turned = matmul_nt(wt[first : first + 256, :], normed[rows, :])
        lanes = pl.ds(pl.multiple_of(quad * 128, 128), 128)
        for h in range(HEADS):
            block = turned[32 * h : 32 * h + 32, :]
            stack = jnp.concatenate([block[:, 128 * s : 128 * s + 128] for s in range(4)], axis=0)
            target[h, :, lanes] = stack.T.astype(BF16)

    def ring_copy(buf, send, recv, way, source, device, u):
        spot = buf.at[source, pair_of(u)]
        return remote(spot, spot, send.at[way, u], recv.at[way, u], device)

    def ring(buf, send, recv, u):
        return (
            ring_copy(buf, send, recv, 0, z, up, u),
            ring_copy(buf, send, recv, 1, z, down, u),
        )

    def onward_up(buf, send, recv, u):
        return ring_copy(buf, send, recv, 2, z_down, up, u)

    def onward_down(buf, send, recv, u):
        return ring_copy(buf, send, recv, 2, z_up, down, u)

    def far_arrived(buf, send, recv, u):
        ring_copy(buf, send, recv, 2, z_far, up, u).wait_recv()

    def ring_forward(buf, send, recv, u):
        @pl.when(lax.rem(u, 2) == 0)
        def _():
            ring_copy(buf, send, recv, 0, z_down, up, u).wait_recv()
            onward_up(buf, send, recv, u).start()
            ring_copy(buf, send, recv, 1, z_up, down, u).wait_recv()

        @pl.when(lax.rem(u, 2) == 1)
        def _():
            ring_copy(buf, send, recv, 1, z_up, down, u).wait_recv()
            onward_down(buf, send, recv, u).start()
            ring_copy(buf, send, recv, 0, z_down, up, u).wait_recv()

    kzs = (kz, kz_s, kz_r)
    vzs = (vz, vz_s, vz_r)

    def first_place(u):
        half = u // 2
        return here * (1 - half) + here_beside * half

    def second_place(u):
        half = u // 2
        return here_beside * (1 - half) + here * half

    def q_copy(way, place, device, u):
        spot = qg.at[place, pair_of(u)]
        return remote(spot, spot, qp_s.at[way, u], qp_r.at[way, u], device)

    def q_twin(u):
        return q_copy(0, first_place(u), twin, u)

    def q_beside(u):
        return q_copy(1, first_place(u), beside, u)

    def q_onward(u):
        return q_copy(2, second_place(u), twin, u)

    def q_peers(u):
        qa.arrived(first_place(u), u, own_q)
        q_beside(u).start()
        q_twin(u).start()

    def q_forward(u):
        q_copy(1, second_place(u), beside, u).wait_recv()
        q_onward(u).start()

    def add_chunk(u):
        far_arrived(*kzs, u)
        half = u // 2
        q_copy(0, here_twin * (1 - half) + here_across * half, twin, u).wait_recv()
        q_copy(2, here_across * (1 - half) + here_twin * half, twin, u).wait_recv()
        keys = [
            jnp.concatenate([kz[zz, 2 * u + i] for zz in range(4)], axis=1) for i in range(2)
        ]
        for p in range(4):
            rows = slice(128 * p, 128 * p + 128)
            term = matmul(qg[p, 2 * u], keys[0]) + matmul(qg[p, 2 * u + 1], keys[1])

            @pl.when(u == 0)
            def _():
                logits[rows, :] = term

            @pl.when(u > 0)
            def _():
                logits[rows, :] += term

    scale = 1.0 / math.sqrt(SEQ_DEVICES * 16 * HEAD_DIM)

    def stat_copy(i, device):
        return remote(stats.at[here], stats.at[here], st_s.at[i], st_r.at[i], device)

    def stat_wait(i, spot):
        remote(stats.at[spot], stats.at[spot], st_s.at[i], st_r.at[i], twin).wait_recv()

    def local_softmax():
        for p in range(4):
            rows = slice(128 * p, 128 * p + 128)
            highest = jnp.max(logits[rows, :], axis=1, keepdims=True)
            expo = jnp.exp((logits[rows, :] - highest) * scale)
            logits[rows, :] = expo
            total = jnp.sum(expo, axis=1, keepdims=True)
            stats[here, 0, :, rows] = jnp.broadcast_to(highest, (128, 128)).T[0:8, :]
            stats[here, 1, :, rows] = jnp.broadcast_to(total, (128, 128)).T[0:8, :]
        stat_copy(1, beside).start()
        stat_copy(2, across).start()
        stat_copy(0, twin).start()

    def finish_softmax():
        stat_wait(0, here_twin)
        stat_wait(1, here_beside)
        stat_wait(2, here_across)
        highest = stats[0, 0]
        for p in range(1, 4):
            highest = jnp.maximum(highest, stats[p, 0])
        total = jnp.zeros((8, 512), F32)
        for p in range(4):
            total += stats[p, 1] * jnp.exp((stats[p, 0] - highest) * scale)
        factor = jnp.exp((stats[here, 0] - highest) * scale) / total
        for p in range(4):
            rows = slice(128 * p, 128 * p + 128)
            column = jnp.broadcast_to(factor[0:1, rows], (128, 128)).T
            for q in range(4):
                lanes = slice(128 * q, 128 * q + 128)
                probs[rows, lanes] = (logits[rows, lanes] * column).astype(BF16)

    def oc(t):
        return remote(oc_s.at[t], oc_r.at[t], oc_ss.at[t], oc_rs.at[t], twin)

    def oy(t):
        return remote(oy_s.at[t], oy_r.at[t], oy_ss.at[t], oy_rs.at[t], beside)

    def attend(u):
        far_arrived(*vzs, u)

        @pl.loop(0, 2)
        def _(i):
            t = 2 * u + i
            slot = lax.rem(t, 4)
            values = jnp.concatenate([vz[zz, t] for zz in range(4)], axis=0)
            for p in range(4):
                o_part[slot, p] = matmul(probs[128 * p : 128 * p + 128, :], values)
            for y in range(2):
                oc_s[t, y] = o_part[slot, 2 * y + 1 - c].astype(BF16)
            oc(t).start()

    same = pl.ds(pl.multiple_of(yh * 64, 64), 64)
    other = pl.ds(pl.multiple_of((1 - yh) * 64, 64), 64)

    def add_twin(u):
        @pl.loop(0, 2)
        def _(i):
            t = 2 * u + i
            slot = lax.rem(t, 4)
            oc(t).wait_recv()
            oy_s[t, 0] = (
                o_part[slot, here, other, :] + oc_r[t, yl, other, :].astype(F32)
            ).astype(BF16)
            oy_s[t, 1] = (
                o_part[slot, here_beside, same, :] + oc_r[t, 1 - yl, same, :].astype(F32)
            ).astype(BF16)
            oy(t).start()

    def column_rows(k):
        column = lax.rem(xx + 4 - k, 4)
        return column, pl.ds(pl.multiple_of(column * 16, 16), 16)

    def oa_near(t, k):
        column, rows = column_rows(k)
        return remote(
            oa_s.at[0, t, rows, :], oh.at[me, t], oa_ss.at[t, k], oa_rs.at[t, k], (yh * 4 + column, res)
        )

    def oa_far(t, k):
        rows = column_rows(k)[1]
        return remote(
            oa_s.at[1, t, rows, :], oh.at[me, t], oa_ss.at[t, 4 + k], oa_rs.at[t, 4 + k], diagonal(k)
        )

    def oa_wait(t, k):
        for far in (0, 1):
            if k == 0 and far == 0:
                continue
            source = lax.rem(yh + far, 2) * 4 + lax.rem(xx + k, 4)
            spot = oh.at[source, t]
            remote(spot, spot, oa_ss.at[t, 4 * far + k], oa_rs.at[t, 4 * far + k], beside).wait_recv()

    def add_beside(u):
        @pl.loop(0, 2)
        def _(i):
            t = 2 * u + i
            slot = lax.rem(t, 4)
            oy(t).wait_recv()
            oa_s[1, t] = (
                o_part[slot, here_beside, other, :]
                + oc_r[t, 1 - yl, other, :].astype(F32)
                + oy_r[t, 0].astype(F32)
            ).astype(BF16)
            for k in (2, 1, 3, 0):
                oa_far(t, k).start()
            oa_s[0, t] = (
                o_part[slot, here, same, :]
                + oc_r[t, yl, same, :].astype(F32)
                + oy_r[t, 1].astype(F32)
            ).astype(BF16)
            for k in (2, 1, 3):
                oa_near(t, k).start()
            oh[me, t] = oa_s[0, t, column_rows(0)[1], :]

    mine = pl.ds(pl.multiple_of(me * 16, 16), 16)
    own_x = pltpu.make_async_copy(x.at[:, mine, :], xc.at[mine], own_s.at[3])

    def x_copy(t):
        g = turn(t)
        return remote(
            x.at[:, pl.ds(pl.multiple_of(g * 16, 16), 16), :], xc.at[mine],
            col_s.at[t], col_r.at[t], (g, res),
        )

    def x_start():
        own_x.start()
        for t in range(1, SEQ_DEVICES):
            x_copy(t).start()

    def x_arrived():
        own_x.wait()
        for t in range(1, SEQ_DEVICES):
            spot = xc.at[pl.ds(pl.multiple_of(unturn(t) * 16, 16), 16)]
            remote(spot, spot, col_s.at[t], col_r.at[t], (turn(t), res)).wait_recv()

    def gate_block(i):
        rows = pl.ds(pl.multiple_of(i * 512, 512), 512)
        entries = xc[pl.ds(pl.multiple_of(i * 32, 32), 32)].reshape(512, 256).astype(F32)
        gates[rows, :] = jax.nn.sigmoid(matmul(layer_normalize(entries).astype(BF16), wg[...]))

    def prepare(i):
        @pl.when(i == 0)
        def _():
            wt[0:256, :] = flip(cq[...])
            swap[...] = swap_matrix()

        @pl.when(i == 1)
        def _():
            wt[256:512, :] = flip(cv[...])
            wt[512:768, :] = flip(cg[...])

        for quarter in range(4):
            picks[quarter, pl.ds(pl.multiple_of(i * 256, 256), 256), :] = pick_matrix(i, quarter)
        wide[i] = jnp.zeros((256, 1024), BF16)

    @pl.loop(0, 4)
    def _(quad):
        project(quad, 256, qs)

    own_q.start()
    qa.start()

    def v_project(u):
        project(2 * u, 512, vs)
        project(2 * u + 1, 512, vs)

        @pl.when(u == 1)
        def _():
            own_v.start()
            va.start()

    def k_own(u):
        ka.arrived(z, u, own_k)
        for copy in ring(*kzs, u):
            copy.start()

    def v_own(u):
        va.arrived(z, u, own_v)
        for copy in ring(*vzs, u):
            copy.start()

    @pl.loop(0, 13)
    def _(tick):
        def during(first, action, count=4):
            @pl.when((tick >= first) & (tick < first + count))
            def _():
                action(tick - first)

        during(9, add_beside)
        during(8, add_twin)
        during(0, k_own)
        during(1, lambda u: ka.forward(), 1)
        during(1, v_project, 2)
        during(3, v_own)
        during(1, lambda u: ring_forward(*kzs, u))
        during(5, lambda u: ring_forward(*vzs, u))
        during(2, lambda u: qa.forward(), 1)
        during(4, lambda u: va.forward(), 1)
        during(1, q_peers)
        during(2, q_forward)
        during(2, prepare, 4)
        during(7, lambda u: x_start(), 1)
        during(3, add_chunk)
        during(6, lambda u: local_softmax(), 1)
        during(7, lambda u: finish_softmax(), 1)
        during(7, attend)
        during(9, lambda u: x_arrived(), 1)
        during(9, gate_block, 4)

    @pl.loop(0, 8)
    def _(t):
        for k in range(4):
            oa_wait(t, k)

    def chunk_of(h, g):
        return (g // 4 - h // 4) % 2 * 4 + (g - h) % 4

    @pl.loop(0, 4)
    def _(quarter):
        stack = jnp.concatenate(
            [
                jnp.concatenate(
                    [
                        jnp.concatenate(
                            [oh[h, chunk_of(h, g), :, 128 * q : 128 * q + 128] for g in range(8)], axis=0
                        )
                        for h in range(HEADS)
                    ],
                    axis=1,
                )
                for q in range(4)
            ],
            axis=0,
        )
        spread = matmul(stack, picks[quarter]).astype(BF16)
        for q in range(4):
            osc[:, 4 * q + quarter] = spread[128 * q : 128 * q + 128, :].reshape(8, 16, 256)

    @pl.loop(0, 8, unroll=4)
    def _(g):
        rows = pl.ds(pl.multiple_of(g * 256, 256), 256)
        update = (gates[rows, :] * osc[g].reshape(256, 256).astype(F32)).astype(BF16)
        entries = xc[pl.ds(pl.multiple_of(g * 16, 16), 16)].reshape(256, 256).astype(F32)
        after = (entries + matmul(update, wf[...])).astype(BF16)
        turned = matmul(swap[...], after).astype(BF16)
        for r in range(16):
            x2[pl.ds(pl.multiple_of(r * 128 + g * 16, 16), 16), :] = turned[16 * r : 16 * r + 16, :]

    col_scale = 1.0 / math.sqrt(HEAD_DIM)

    def result(block, t):
        g = turn(t)
        return remote(
            done.at[pl.ds(block * 4, 4), pl.ds(pl.multiple_of(g * 16, 16), 16), :],
            out.at[pl.ds(me * 16 + block * 4, 4)],
            back_s.at[block, t], back_r.at[block, t], (g, res),
        )

    @pl.loop(0, 4)
    def _(block):
        rows = pl.ds(pl.multiple_of(block * 512, 512), 512)
        entries = x2[rows, :].astype(F32)
        part = layer_normalize(entries).astype(BF16)
        keys = matmul(part, ck[...]).astype(BF16)
        turned = matmul_nt(wt[...], part)
        queries = turned[0:256, :].astype(BF16)
        values = turned[256:512, :].astype(BF16)
        gate = jax.nn.sigmoid(turned[512:768, :])
        updates = []
        for r in range(4):
            lanes = slice(128 * r, 128 * r + 128)
            for h in range(HEADS):
                wide[r, 32 * h : 32 * h + 32, 128 * h : 128 * h + 128] = queries[
                    32 * h : 32 * h + 32, lanes
                ]
            scores = matmul(keys[lanes, :], wide[r])
            highest = jnp.max(scores, axis=0, keepdims=True)
            expo = jnp.exp((scores - highest) * col_scale)
            total = jnp.sum(expo, axis=0, keepdims=True)
            weights = (expo * (1.0 / total)).astype(BF16)
            mixed = []
            for h in range(0, HEADS, 2):
                both = matmul(values[32 * h : 32 * h + 64, lanes], weights[:, 128 * h : 128 * h + 256])
                mixed += [both[0:32, 0:128], both[32:64, 128:256]]
            mixed = jnp.concatenate(mixed, axis=0)
            updates.append((gate[:, lanes] * mixed).astype(BF16).astype(F32).T.astype(BF16))
        update = jnp.concatenate(updates, axis=0)
        after = (entries + matmul(update, cf[...])).astype(BF16).astype(F32)
        hidden = matmul(layer_normalize(after).astype(BF16), ce[...])
        hidden = jnp.maximum(hidden, 0.0).astype(BF16)
        total = (after + matmul(hidden, cs[...])).astype(BF16)
        for r in range(4):
            done[block * 4 + r] = total[128 * r : 128 * r + 128, :]
        for t in range(1, SEQ_DEVICES):
            result(block, t).start()

    out[pl.ds(pl.multiple_of(me * 16, 16), 16)] = done[:, mine, :]

    for exchange in (ka, qa, va):
        exchange.drain()
    stat_copy(0, twin).wait_send()
    stat_copy(1, beside).wait_send()
    stat_copy(2, across).wait_send()

    @pl.loop(0, 4)
    def _(u):
        for buf in (kzs, vzs):
            for copy in ring(*buf, u):
                copy.wait_send()

            @pl.when(lax.rem(u, 2) == 0)
            def _():
                onward_up(*buf, u).wait_send()

            @pl.when(lax.rem(u, 2) == 1)
            def _():
                onward_down(*buf, u).wait_send()

        q_twin(u).wait_send()
        q_beside(u).wait_send()
        q_onward(u).wait_send()

    @pl.loop(0, 8)
    def _(t):
        oc(t).wait_send()
        oy(t).wait_send()
        for k in range(4):
            oa_far(t, k).wait_send()
        for k in range(1, 4):
            oa_near(t, k).wait_send()

    for t in range(1, SEQ_DEVICES):
        x_copy(t).wait_send()

    @pl.loop(1, 8)
    def _(t):
        g = unturn(t)
        for block in range(4):
            spot = out.at[pl.ds(g * 16 + block * 4, 4)]
            remote(spot, spot, back_s.at[block, t], back_r.at[block, t], (turn(t), res)).wait_recv()

    @pl.loop(1, 8)
    def _(t):
        for block in range(4):
            result(block, t).wait_send()


def on_device(
    homolog_tensor,
    horizontal_probe_matrix,
    horizontal_lookup_matrix,
    horizontal_payload_matrix,
    horizontal_sigmoid_matrix,
    horizontal_final_matrix,
    vertical_probe_matrix,
    vertical_lookup_matrix,
    vertical_payload_matrix,
    vertical_sigmoid_matrix,
    vertical_final_matrix,
    expanding_matrix,
    shrinking_matrix,
):
    dma = pltpu.SemaphoreType.DMA
    vmem = pltpu.VMEM
    columns = pl.pallas_call(
        kernel,
        name="msa_block",
        out_shape=jax.ShapeDtypeStruct((128, 16, 256), BF16),
        in_specs=[pl.BlockSpec(memory_space=vmem)] * 13,
        out_specs=pl.BlockSpec(memory_space=vmem),
        scratch_shapes=[
            vmem((2048, 256), BF16),
            vmem((768, 256), BF16),
            vmem((8, 512, 128), BF16),
            vmem((8, 128, 512), BF16),
            vmem((8, 128, 512), BF16),
            vmem((4, 512, 128), BF16),
            vmem((4, 128, 512), BF16),
            vmem((4, 128, 512), BF16),
            vmem((4, 8, 512, 128), BF16),
            vmem((4, 8, 128, 512), BF16),
            vmem((4, 8, 128, 512), BF16),
            vmem((512, 512), F32),
            vmem((512, 512), BF16),
            vmem((4, 2, 8, 512), F32),
            vmem((4, 4, 128, 512), F32),
            vmem((8, 2, 128, 512), BF16),
            vmem((8, 2, 128, 512), BF16),
            vmem((8, 2, 64, 512), BF16),
            vmem((8, 2, 64, 512), BF16),
            vmem((2, 8, 64, 512), BF16),
            vmem((8, 8, 16, 512), BF16),
            vmem((128, 16, 256), BF16),
            vmem((2048, 256), F32),
            vmem((4, 1024, 256), BF16),
            vmem((8, 16, 16, 256), BF16),
            vmem((256, 256), BF16),
            vmem((2048, 256), BF16),
            vmem((4, 256, 1024), BF16),
            vmem((16, 128, 256), BF16),
        ]
        + [dma((3, 4))] * 6
        + [dma((3, 4))] * 6
        + [dma((3,))] * 2
        + [dma((8,))] * 4
        + [dma((8, 8))] * 2
        + [dma((8,))] * 2
        + [dma((4, 8))] * 2
        + [dma((4,))],
        compiler_params=pltpu.CompilerParams(
            collective_id=0, has_side_effects=True, vmem_limit_bytes=62 * 2**20
        ),
    )(
        homolog_tensor,
        horizontal_probe_matrix,
        horizontal_lookup_matrix,
        horizontal_payload_matrix,
        horizontal_sigmoid_matrix,
        horizontal_final_matrix,
        vertical_probe_matrix,
        vertical_lookup_matrix,
        vertical_payload_matrix,
        vertical_sigmoid_matrix,
        vertical_final_matrix,
        expanding_matrix,
        shrinking_matrix,
    )
    return jnp.transpose(columns, (1, 0, 2))


def solution(mesh):
    in_specs = (P("seq", "res", None), P(), P(), P(), P(), P(), P(), P(), P(), P(), P(), P(), P())
    out_specs = P("seq", "res", None)
    return jax.shard_map(
        on_device, mesh=mesh, in_specs=in_specs, out_specs=out_specs, check_vma=False
    )
```

```python
import math

import jax
import jax.numpy as jnp
from jax import lax
from jax.experimental import pallas as pl
from jax.experimental.pallas import tpu as pltpu
from jax.sharding import PartitionSpec as P

HEADS = 8
HEAD_DIM = 32
SEQ_DEVICES = 8
MESH = pl.DeviceIdType.MESH
BF16 = jnp.bfloat16
F32 = jnp.float32
NT = (((1,), (1,)), ((), ()))


def layer_normalize(entries):
    center = entries - jnp.mean(entries, axis=-1, keepdims=True)
    spread = jnp.mean(center * center, axis=-1, keepdims=True)
    return center * lax.rsqrt(spread + 1e-05)


def matmul(a, b):
    return jnp.dot(a, b, preferred_element_type=F32)


def matmul_nt(a, b):
    return lax.dot_general(a, b, NT, preferred_element_type=F32)


def flip(a):
    return a.astype(F32).T.astype(BF16)


def remote(src, dst, send, recv, device):
    return pltpu.make_async_remote_copy(
        src_ref=src, dst_ref=dst, send_sem=send, recv_sem=recv, device_id=device, device_id_type=MESH
    )


class Exchange:
    def __init__(self, place, src, dst, mid, slot, send, recv, onward_device, direct):
        self.yh, self.xx, self.me, self.res = place
        self.src, self.dst, self.mid, self.slot = src, dst, mid, slot
        self.send, self.recv = send, recv
        self.onward_device, self.direct = onward_device, direct

    def near(self, k):
        to = self.yh * 4 + lax.rem(self.xx + 4 - k, 4)
        return remote(
            self.src.at[to], self.dst.at[self.slot, k],
            self.send.at[0, k], self.recv.at[0, k], (to, self.res),
        )

    def far(self, k):
        column = lax.rem(self.xx + 4 - k, 4)
        return remote(
            self.src.at[(1 - self.yh) * 4 + column], self.mid.at[k],
            self.send.at[1, k], self.recv.at[1, k], (self.yh * 4 + column, self.res),
        )

    def onward(self, k):
        column = self.xx
        src = self.mid.at[k]
        if k == 0 or self.direct:
            column = lax.rem(self.xx + 4 - k, 4)
            src = self.src.at[(1 - self.yh) * 4 + column]
        return remote(
            src, self.dst.at[self.slot, 4 + k], self.send.at[2, k], self.recv.at[2, k],
            ((1 - self.yh) * 4 + column, self.onward_device[1]),
        )

    def start(self):
        for k in (1, 3, 2):
            self.near(k).start()
        self.onward(0).start()
        for k in (1, 3, 2):
            if self.direct:
                self.onward(k).start()
            else:
                self.far(k).start()

    def forward(self):
        for k in () if self.direct else (1, 3, 2):
            self.far(k).wait_recv()
            self.onward(k).start()

    def arrived(self, place, pair, own):
        def wait(leg, k, t):
            spot = self.dst.at[place, t]
            remote(spot, spot, self.send.at[leg, k], self.recv.at[leg, k], self.onward_device).wait_recv()

        @pl.when(pair == 0)
        def _():
            own.wait()
            wait(0, 1, 1)

        @pl.when(pair == 1)
        def _():
            wait(0, 2, 2)
            wait(0, 3, 3)

        @pl.when(pair >= 2)
        def _():
            wait(2, 2 * pair - 4, 2 * pair)
            wait(2, 2 * pair - 3, 2 * pair + 1)

    def drain(self):
        for k in range(1, 4):
            self.near(k).wait_send()
            if not self.direct:
                self.far(k).wait_send()
        for k in range(4):
            self.onward(k).wait_send()


def swap_matrix():
    a = lax.broadcasted_iota(jnp.int32, (256, 256), 0)
    b = lax.broadcasted_iota(jnp.int32, (256, 256), 1)
    return jnp.where(b == ((a & 15) << 4) + (a >> 4), 1.0, 0.0).astype(BF16)


def pick_matrix(block, quarter):
    k = lax.broadcasted_iota(jnp.int32, (256, 256), 0) + block * 256
    n = lax.broadcasted_iota(jnp.int32, (256, 256), 1)
    same = ((k >> 7) == (n >> 5)) & (((k >> 5) & 3) == quarter) & ((k & 31) == (n & 31))
    return jnp.where(same, 1.0, 0.0).astype(BF16)


def kernel(
    x_in, wq_in, wk_in, wv_in, wg_in, wf_in, cq_in, ck_in, cv_in, cg_in, cf_in, ce_in, cs_in, out,
    x, wq, wk, wv, wg, wf, cq, ck, cv, cg, cf, ce, cs,
    normed, wt, ks, qs, vs, kmid, qmid, vmid, kz, vz, qg, logits, probs, stats,
    o_part, oc_s, oc_r, oy_s, oy_r, oa_s, oh, xc, gates, picks, osc,
    swap, x2, wide, done,
    ka_s, ka_r, qa_s, qa_r, va_s, va_r, kz_s, kz_r, vz_s, vz_r, qp_s, qp_r,
    st_s, st_r, oc_ss, oc_rs, oy_ss, oy_rs, oa_ss, oa_rs, col_s, col_r, back_s, back_r, own_s, load_s,
):
    me = lax.axis_index("seq")
    res = lax.axis_index("res")
    z = res // 4
    yl = lax.rem(res // 2, 2)
    c = lax.rem(res, 2)
    here = lax.rem(res, 4)
    yh = me // 4
    xx = lax.rem(me, 4)

    def at_res(zz, yy, cc):
        return (me, zz * 4 + yy * 2 + cc)

    z_up = lax.rem(z + 1, 4)
    z_down = lax.rem(z + 3, 4)
    z_far = lax.rem(z + 2, 4)
    up = at_res(z_up, yl, c)
    down = at_res(z_down, yl, c)
    twin = at_res(z, yl, 1 - c)
    beside = at_res(z, 1 - yl, c)
    across = at_res(z, 1 - yl, 1 - c)
    res_beside = z * 4 + (1 - yl) * 2 + c
    opposite = ((1 - yh) * 4 + xx, res)
    here_twin = yl * 2 + (1 - c)
    here_beside = (1 - yl) * 2 + c
    here_across = (1 - yl) * 2 + (1 - c)

    def diagonal(k):
        return ((1 - yh) * 4 + lax.rem(xx + 4 - k, 4), res_beside)

    def pair_of(u):
        return pl.ds(u * 2, 2)

    def turn(t):
        return lax.rem(me + t, SEQ_DEVICES)

    def unturn(t):
        return lax.rem(me + SEQ_DEVICES - t, SEQ_DEVICES)

    barrier = pltpu.get_barrier_semaphore()
    partners = [(turn(t), res) for t in range(1, SEQ_DEVICES)] + [up, down, twin, beside, across]
    partners += [diagonal(k) for k in range(4)]
    for device in partners:
        pl.semaphore_signal(barrier, inc=1, device_id=device, device_id_type=MESH)

    loads = [
        pltpu.make_async_copy(source, target, load_s.at[i])
        for i, (source, target) in enumerate(
            (
                (x_in, x), (wk_in, wk), (wq_in, wq), (wv_in, wv), (wg_in, wg), (wf_in, wf), (cq_in, cq),
                (ck_in, ck), (cv_in, cv), (cg_in, cg), (cf_in, cf), (ce_in, ce), (cs_in, cs),
            )
        )
    ]
    for load in loads:
        load.start()
    loads[1].wait()
    wt[0:256, :] = flip(wk[...])
    loads[0].wait()

    @pl.loop(0, 4)
    def _(quad):
        rows = pl.ds(pl.multiple_of(quad * 512, 512), 512)
        entries = x[pl.ds(quad * 4, 4)].reshape(512, 256)
        part = layer_normalize(entries.astype(F32)).astype(BF16)
        normed[rows, :] = part
        keys = matmul_nt(wt[0:256, :], part).astype(BF16)
        for h in range(HEADS):
            for s in range(4):
                place = pl.ds(pl.multiple_of(quad * 128 + 32 * s, 32), 32)
                ks[h, place, :] = keys[32 * h : 32 * h + 32, 128 * s : 128 * s + 128]

    pl.semaphore_wait(barrier, len(partners))

    place = (yh, xx, me, res)
    ka = Exchange(place, ks, kz, kmid, z, ka_s, ka_r, opposite, True)
    va = Exchange(place, vs, vz, vmid, z, va_s, va_r, opposite, False)
    qa = Exchange(place, qs, qg, qmid, here, qa_s, qa_r, diagonal(0), False)

    own_k = pltpu.make_async_copy(ks.at[me], kz.at[z, 0], own_s.at[0])
    own_q = pltpu.make_async_copy(qs.at[me], qg.at[here, 0], own_s.at[1])
    own_v = pltpu.make_async_copy(vs.at[me], vz.at[z, 0], own_s.at[2])
    own_k.start()
    ka.start()

    for load in loads[2:]:
        load.wait()
    wt[256:512, :] = flip(wq[...])
    wt[512:768, :] = flip(wv[...])

    def project(quad, first, target):
        rows = pl.ds(pl.multiple_of(quad * 512, 512), 512)
        turned = matmul_nt(wt[first : first + 256, :], normed[rows, :])
        lanes = pl.ds(pl.multiple_of(quad * 128, 128), 128)
        for h in range(HEADS):
            block = turned[32 * h : 32 * h + 32, :]
            stack = jnp.concatenate([block[:, 128 * s : 128 * s + 128] for s in range(4)], axis=0)
            target[h, :, lanes] = stack.T.astype(BF16)

    def ring_copy(buf, send, recv, way, source, device, u):
        spot = buf.at[source, pair_of(u)]
        return remote(spot, spot, send.at[way, u], recv.at[way, u], device)

    def ring(buf, send, recv, u):
        return (
            ring_copy(buf, send, recv, 0, z, up, u),
            ring_copy(buf, send, recv, 1, z, down, u),
        )

    def onward_up(buf, send, recv, u):
        return ring_copy(buf, send, recv, 2, z_down, up, u)

    def onward_down(buf, send, recv, u):
        return ring_copy(buf, send, recv, 2, z_up, down, u)

    def far_arrived(buf, send, recv, u):
        ring_copy(buf, send, recv, 2, z_far, up, u).wait_recv()

    def ring_forward(buf, send, recv, u):
        @pl.when(lax.rem(u, 2) == 0)
        def _():
            ring_copy(buf, send, recv, 0, z_down, up, u).wait_recv()
            onward_up(buf, send, recv, u).start()
            ring_copy(buf, send, recv, 1, z_up, down, u).wait_recv()

        @pl.when(lax.rem(u, 2) == 1)
        def _():
            ring_copy(buf, send, recv, 1, z_up, down, u).wait_recv()
            onward_down(buf, send, recv, u).start()
            ring_copy(buf, send, recv, 0, z_down, up, u).wait_recv()

    kzs = (kz, kz_s, kz_r)
    vzs = (vz, vz_s, vz_r)

    def first_place(u):
        half = u // 2
        return here * (1 - half) + here_beside * half

    def second_place(u):
        half = u // 2
        return here_beside * (1 - half) + here * half

    def q_copy(way, place, device, u):
        spot = qg.at[place, pair_of(u)]
        return remote(spot, spot, qp_s.at[way, u], qp_r.at[way, u], device)

    def q_twin(u):
        return q_copy(0, first_place(u), twin, u)

    def q_beside(u):
        return q_copy(1, first_place(u), beside, u)

    def q_onward(u):
        return q_copy(2, second_place(u), twin, u)

    def q_peers(u):
        qa.arrived(first_place(u), u, own_q)
        q_beside(u).start()
        q_twin(u).start()

    def q_forward(u):
        q_copy(1, second_place(u), beside, u).wait_recv()
        q_onward(u).start()

    def add_chunk(u):
        far_arrived(*kzs, u)
        half = u // 2
        q_copy(0, here_twin * (1 - half) + here_across * half, twin, u).wait_recv()
        q_copy(2, here_across * (1 - half) + here_twin * half, twin, u).wait_recv()
        keys = [
            jnp.concatenate([kz[zz, 2 * u + i] for zz in range(4)], axis=1) for i in range(2)
        ]
        for p in range(4):
            rows = slice(128 * p, 128 * p + 128)
            term = matmul(qg[p, 2 * u], keys[0]) + matmul(qg[p, 2 * u + 1], keys[1])

            @pl.when(u == 0)
            def _():
                logits[rows, :] = term

            @pl.when(u > 0)
            def _():
                logits[rows, :] += term

    scale = 1.0 / math.sqrt(SEQ_DEVICES * 16 * HEAD_DIM)

    def stat_copy(i, device):
        return remote(stats.at[here], stats.at[here], st_s.at[i], st_r.at[i], device)

    def stat_wait(i, spot):
        remote(stats.at[spot], stats.at[spot], st_s.at[i], st_r.at[i], twin).wait_recv()

    def local_softmax():
        for p in range(4):
            rows = slice(128 * p, 128 * p + 128)
            highest = jnp.max(logits[rows, :], axis=1, keepdims=True)
            expo = jnp.exp((logits[rows, :] - highest) * scale)
            logits[rows, :] = expo
            total = jnp.sum(expo, axis=1, keepdims=True)
            stats[here, 0, :, rows] = jnp.broadcast_to(highest, (128, 128)).T[0:8, :]
            stats[here, 1, :, rows] = jnp.broadcast_to(total, (128, 128)).T[0:8, :]
        stat_copy(1, beside).start()
        stat_copy(2, across).start()
        stat_copy(0, twin).start()

    def finish_softmax():
        stat_wait(0, here_twin)
        stat_wait(1, here_beside)
        stat_wait(2, here_across)
        highest = stats[0, 0]
        for p in range(1, 4):
            highest = jnp.maximum(highest, stats[p, 0])
        total = jnp.zeros((8, 512), F32)
        for p in range(4):
            total += stats[p, 1] * jnp.exp((stats[p, 0] - highest) * scale)
        factor = jnp.exp((stats[here, 0] - highest) * scale) / total
        for p in range(4):
            rows = slice(128 * p, 128 * p + 128)
            column = jnp.broadcast_to(factor[0:1, rows], (128, 128)).T
            for q in range(4):
                lanes = slice(128 * q, 128 * q + 128)
                probs[rows, lanes] = (logits[rows, lanes] * column).astype(BF16)

    def oc(t):
        return remote(oc_s.at[t], oc_r.at[t], oc_ss.at[t], oc_rs.at[t], twin)

    def oy(t):
        return remote(oy_s.at[t], oy_r.at[t], oy_ss.at[t], oy_rs.at[t], beside)

    def attend(u):
        far_arrived(*vzs, u)

        @pl.loop(0, 2)
        def _(i):
            t = 2 * u + i
            slot = lax.rem(t, 4)
            values = jnp.concatenate([vz[zz, t] for zz in range(4)], axis=0)
            for p in range(4):
                o_part[slot, p] = matmul(probs[128 * p : 128 * p + 128, :], values)
            for y in range(2):
                oc_s[t, y] = o_part[slot, 2 * y + 1 - c].astype(BF16)
            oc(t).start()

    same = pl.ds(pl.multiple_of(yh * 64, 64), 64)
    other = pl.ds(pl.multiple_of((1 - yh) * 64, 64), 64)

    def add_twin(u):
        @pl.loop(0, 2)
        def _(i):
            t = 2 * u + i
            slot = lax.rem(t, 4)
            oc(t).wait_recv()
            oy_s[t, 0] = (
                o_part[slot, here, other, :] + oc_r[t, yl, other, :].astype(F32)
            ).astype(BF16)
            oy_s[t, 1] = (
                o_part[slot, here_beside, same, :] + oc_r[t, 1 - yl, same, :].astype(F32)
            ).astype(BF16)
            oy(t).start()

    def column_rows(k):
        column = lax.rem(xx + 4 - k, 4)
        return column, pl.ds(pl.multiple_of(column * 16, 16), 16)

    def oa_near(t, k):
        column, rows = column_rows(k)
        return remote(
            oa_s.at[0, t, rows, :], oh.at[me, t], oa_ss.at[t, k], oa_rs.at[t, k], (yh * 4 + column, res)
        )

    def oa_far(t, k):
        rows = column_rows(k)[1]
        return remote(
            oa_s.at[1, t, rows, :], oh.at[me, t], oa_ss.at[t, 4 + k], oa_rs.at[t, 4 + k], diagonal(k)
        )

    def oa_wait(t, k):
        for far in (0, 1):
            if k == 0 and far == 0:
                continue
            source = lax.rem(yh + far, 2) * 4 + lax.rem(xx + k, 4)
            spot = oh.at[source, t]
            remote(spot, spot, oa_ss.at[t, 4 * far + k], oa_rs.at[t, 4 * far + k], beside).wait_recv()

    def add_beside(u):
        @pl.loop(0, 2)
        def _(i):
            t = 2 * u + i
            slot = lax.rem(t, 4)
            oy(t).wait_recv()
            oa_s[1, t] = (
                o_part[slot, here_beside, other, :]
                + oc_r[t, 1 - yl, other, :].astype(F32)
                + oy_r[t, 0].astype(F32)
            ).astype(BF16)
            for k in (2, 1, 3, 0):
                oa_far(t, k).start()
            oa_s[0, t] = (
                o_part[slot, here, same, :]
                + oc_r[t, yl, same, :].astype(F32)
                + oy_r[t, 1].astype(F32)
            ).astype(BF16)
            for k in (2, 1, 3):
                oa_near(t, k).start()
            oh[me, t] = oa_s[0, t, column_rows(0)[1], :]

    mine = pl.ds(pl.multiple_of(me * 16, 16), 16)
    own_x = pltpu.make_async_copy(x.at[:, mine, :], xc.at[mine], own_s.at[3])

    def x_copy(t):
        g = turn(t)
        return remote(
            x.at[:, pl.ds(pl.multiple_of(g * 16, 16), 16), :], xc.at[mine],
            col_s.at[t], col_r.at[t], (g, res),
        )

    def x_start():
        own_x.start()
        for t in range(1, SEQ_DEVICES):
            x_copy(t).start()

    def x_arrived():
        own_x.wait()
        for t in range(1, SEQ_DEVICES):
            spot = xc.at[pl.ds(pl.multiple_of(unturn(t) * 16, 16), 16)]
            remote(spot, spot, col_s.at[t], col_r.at[t], (turn(t), res)).wait_recv()

    def gate_block(i):
        rows = pl.ds(pl.multiple_of(i * 512, 512), 512)
        entries = xc[pl.ds(pl.multiple_of(i * 32, 32), 32)].reshape(512, 256).astype(F32)
        gates[rows, :] = jax.nn.sigmoid(matmul(layer_normalize(entries).astype(BF16), wg[...]))

    def prepare(i):
        @pl.when(i == 0)
        def _():
            wt[0:256, :] = flip(cq[...])
            swap[...] = swap_matrix()

        @pl.when(i == 1)
        def _():
            wt[256:512, :] = flip(cv[...])
            wt[512:768, :] = flip(cg[...])

        for quarter in range(4):
            picks[quarter, pl.ds(pl.multiple_of(i * 256, 256), 256), :] = pick_matrix(i, quarter)
        wide[i] = jnp.zeros((256, 1024), BF16)

    @pl.loop(0, 4)
    def _(quad):
        project(quad, 256, qs)

    own_q.start()
    qa.start()

    def v_project(u):
        project(2 * u, 512, vs)
        project(2 * u + 1, 512, vs)

        @pl.when(u == 1)
        def _():
            own_v.start()
            va.start()

    def k_own(u):
        ka.arrived(z, u, own_k)
        for copy in ring(*kzs, u):
            copy.start()

    def v_own(u):
        va.arrived(z, u, own_v)
        for copy in ring(*vzs, u):
            copy.start()

    @pl.loop(0, 13)
    def _(tick):
        def during(first, action, count=4):
            @pl.when((tick >= first) & (tick < first + count))
            def _():
                action(tick - first)

        during(0, k_own)
        during(1, lambda u: ka.forward(), 1)
        during(1, v_project, 2)
        during(3, v_own)
        during(1, lambda u: ring_forward(*kzs, u))
        during(5, lambda u: ring_forward(*vzs, u))
        during(9, add_beside)
        during(8, add_twin)
        during(2, lambda u: qa.forward(), 1)
        during(4, lambda u: va.forward(), 1)
        during(1, q_peers)
        during(2, q_forward)
        during(2, prepare, 4)
        during(7, lambda u: x_start(), 1)
        during(3, add_chunk)
        during(6, lambda u: local_softmax(), 1)
        during(7, lambda u: finish_softmax(), 1)
        during(7, attend)
        during(9, lambda u: x_arrived(), 1)
        during(9, gate_block, 4)

    @pl.loop(0, 8)
    def _(t):
        for k in range(4):
            oa_wait(t, k)

    def chunk_of(h, g):
        return (g // 4 - h // 4) % 2 * 4 + (g - h) % 4

    @pl.loop(0, 4)
    def _(quarter):
        stack = jnp.concatenate(
            [
                jnp.concatenate(
                    [
                        jnp.concatenate(
                            [oh[h, chunk_of(h, g), :, 128 * q : 128 * q + 128] for g in range(8)], axis=0
                        )
                        for h in range(HEADS)
                    ],
                    axis=1,
                )
                for q in range(4)
            ],
            axis=0,
        )
        spread = matmul(stack, picks[quarter]).astype(BF16)
        for q in range(4):
            osc[:, 4 * q + quarter] = spread[128 * q : 128 * q + 128, :].reshape(8, 16, 256)

    @pl.loop(0, 8, unroll=4)
    def _(g):
        rows = pl.ds(pl.multiple_of(g * 256, 256), 256)
        update = (gates[rows, :] * osc[g].reshape(256, 256).astype(F32)).astype(BF16)
        entries = xc[pl.ds(pl.multiple_of(g * 16, 16), 16)].reshape(256, 256).astype(F32)
        after = (entries + matmul(update, wf[...])).astype(BF16)
        turned = matmul(swap[...], after).astype(BF16)
        for r in range(16):
            x2[pl.ds(pl.multiple_of(r * 128 + g * 16, 16), 16), :] = turned[16 * r : 16 * r + 16, :]

    col_scale = 1.0 / math.sqrt(HEAD_DIM)

    def result(block, t):
        g = turn(t)
        return remote(
            done.at[pl.ds(block * 4, 4), pl.ds(pl.multiple_of(g * 16, 16), 16), :],
            out.at[pl.ds(me * 16 + block * 4, 4)],
            back_s.at[block, t], back_r.at[block, t], (g, res),
        )

    @pl.loop(0, 4)
    def _(block):
        rows = pl.ds(pl.multiple_of(block * 512, 512), 512)
        entries = x2[rows, :].astype(F32)
        part = layer_normalize(entries).astype(BF16)
        keys = matmul(part, ck[...]).astype(BF16)
        turned = matmul_nt(wt[...], part)
        queries = turned[0:256, :].astype(BF16)
        values = turned[256:512, :].astype(BF16)
        gate = jax.nn.sigmoid(turned[512:768, :])
        updates = []
        for r in range(4):
            lanes = slice(128 * r, 128 * r + 128)
            for h in range(HEADS):
                wide[r, 32 * h : 32 * h + 32, 128 * h : 128 * h + 128] = queries[
                    32 * h : 32 * h + 32, lanes
                ]
            scores = matmul(keys[lanes, :], wide[r])
            highest = jnp.max(scores, axis=0, keepdims=True)
            expo = jnp.exp((scores - highest) * col_scale)
            total = jnp.sum(expo, axis=0, keepdims=True)
            weights = (expo * (1.0 / total)).astype(BF16)
            mixed = []
            for h in range(0, HEADS, 2):
                both = matmul(values[32 * h : 32 * h + 64, lanes], weights[:, 128 * h : 128 * h + 256])
                mixed += [both[0:32, 0:128], both[32:64, 128:256]]
            mixed = jnp.concatenate(mixed, axis=0)
            updates.append((gate[:, lanes] * mixed).astype(BF16).astype(F32).T.astype(BF16))
        update = jnp.concatenate(updates, axis=0)
        after = (entries + matmul(update, cf[...])).astype(BF16).astype(F32)
        hidden = matmul(layer_normalize(after).astype(BF16), ce[...])
        hidden = jnp.maximum(hidden, 0.0).astype(BF16)
        total = (after + matmul(hidden, cs[...])).astype(BF16)
        for r in range(4):
            done[block * 4 + r] = total[128 * r : 128 * r + 128, :]
        for t in range(1, SEQ_DEVICES):
            result(block, t).start()

    out[pl.ds(pl.multiple_of(me * 16, 16), 16)] = done[:, mine, :]

    for exchange in (ka, qa, va):
        exchange.drain()
    stat_copy(0, twin).wait_send()
    stat_copy(1, beside).wait_send()
    stat_copy(2, across).wait_send()

    @pl.loop(0, 4)
    def _(u):
        for buf in (kzs, vzs):
            for copy in ring(*buf, u):
                copy.wait_send()

            @pl.when(lax.rem(u, 2) == 0)
            def _():
                onward_up(*buf, u).wait_send()

            @pl.when(lax.rem(u, 2) == 1)
            def _():
                onward_down(*buf, u).wait_send()

        q_twin(u).wait_send()
        q_beside(u).wait_send()
        q_onward(u).wait_send()

    @pl.loop(0, 8)
    def _(t):
        oc(t).wait_send()
        oy(t).wait_send()
        for k in range(4):
            oa_far(t, k).wait_send()
        for k in range(1, 4):
            oa_near(t, k).wait_send()

    for t in range(1, SEQ_DEVICES):
        x_copy(t).wait_send()

    @pl.loop(1, 8)
    def _(t):
        g = unturn(t)
        for block in range(4):
            spot = out.at[pl.ds(g * 16 + block * 4, 4)]
            remote(spot, spot, back_s.at[block, t], back_r.at[block, t], (turn(t), res)).wait_recv()

    @pl.loop(1, 8)
    def _(t):
        for block in range(4):
            result(block, t).wait_send()


def on_device(
    homolog_tensor,
    horizontal_probe_matrix,
    horizontal_lookup_matrix,
    horizontal_payload_matrix,
    horizontal_sigmoid_matrix,
    horizontal_final_matrix,
    vertical_probe_matrix,
    vertical_lookup_matrix,
    vertical_payload_matrix,
    vertical_sigmoid_matrix,
    vertical_final_matrix,
    expanding_matrix,
    shrinking_matrix,
):
    dma = pltpu.SemaphoreType.DMA
    vmem = pltpu.VMEM
    columns = pl.pallas_call(
        kernel,
        name="msa_block",
        out_shape=jax.ShapeDtypeStruct((128, 16, 256), BF16),
        in_specs=[pl.BlockSpec(memory_space=pl.ANY)] * 13,
        out_specs=pl.BlockSpec(memory_space=vmem),
        scratch_shapes=[vmem((16, 128, 256), BF16)]
        + [vmem((256, 256), BF16)] * 10
        + [vmem((256, 1024), BF16), vmem((1024, 256), BF16)]
        + [
            vmem((2048, 256), BF16),
            vmem((768, 256), BF16),
            vmem((8, 512, 128), BF16),
            vmem((8, 128, 512), BF16),
            vmem((8, 128, 512), BF16),
            vmem((4, 512, 128), BF16),
            vmem((4, 128, 512), BF16),
            vmem((4, 128, 512), BF16),
            vmem((4, 8, 512, 128), BF16),
            vmem((4, 8, 128, 512), BF16),
            vmem((4, 8, 128, 512), BF16),
            vmem((512, 512), F32),
            vmem((512, 512), BF16),
            vmem((4, 2, 8, 512), F32),
            vmem((4, 4, 128, 512), F32),
            vmem((8, 2, 128, 512), BF16),
            vmem((8, 2, 128, 512), BF16),
            vmem((8, 2, 64, 512), BF16),
            vmem((8, 2, 64, 512), BF16),
            vmem((2, 8, 64, 512), BF16),
            vmem((8, 8, 16, 512), BF16),
            vmem((128, 16, 256), BF16),
            vmem((2048, 256), F32),
            vmem((4, 1024, 256), BF16),
            vmem((8, 16, 16, 256), BF16),
            vmem((256, 256), BF16),
            vmem((2048, 256), BF16),
            vmem((4, 256, 1024), BF16),
            vmem((16, 128, 256), BF16),
        ]
        + [dma((3, 4))] * 6
        + [dma((3, 4))] * 6
        + [dma((3,))] * 2
        + [dma((8,))] * 4
        + [dma((8, 8))] * 2
        + [dma((8,))] * 2
        + [dma((4, 8))] * 2
        + [dma((4,))]
        + [dma((13,))],
        compiler_params=pltpu.CompilerParams(
            collective_id=0, has_side_effects=True, vmem_limit_bytes=62 * 2**20
        ),
    )(
        homolog_tensor,
        horizontal_probe_matrix,
        horizontal_lookup_matrix,
        horizontal_payload_matrix,
        horizontal_sigmoid_matrix,
        horizontal_final_matrix,
        vertical_probe_matrix,
        vertical_lookup_matrix,
        vertical_payload_matrix,
        vertical_sigmoid_matrix,
        vertical_final_matrix,
        expanding_matrix,
        shrinking_matrix,
    )
    return jnp.transpose(columns, (1, 0, 2))


def solution(mesh):
    in_specs = (P("seq", "res", None), P(), P(), P(), P(), P(), P(), P(), P(), P(), P(), P(), P())
    out_specs = P("seq", "res", None)
    return jax.shard_map(
        on_device, mesh=mesh, in_specs=in_specs, out_specs=out_specs, check_vma=False
    )
```

```python
import math

import jax
import jax.numpy as jnp
from jax import lax
from jax.experimental import pallas as pl
from jax.experimental.pallas import tpu as pltpu
from jax.sharding import PartitionSpec as P

HEADS = 8
HEAD_DIM = 32
SEQ_DEVICES = 8
MESH = pl.DeviceIdType.MESH
BF16 = jnp.bfloat16
F32 = jnp.float32
NT = (((1,), (1,)), ((), ()))


def layer_normalize(entries):
    center = entries - jnp.mean(entries, axis=-1, keepdims=True)
    spread = jnp.mean(center * center, axis=-1, keepdims=True)
    return center * lax.rsqrt(spread + 1e-05)


def matmul(a, b):
    return jnp.dot(a, b, preferred_element_type=F32)


def matmul_nt(a, b):
    return lax.dot_general(a, b, NT, preferred_element_type=F32)


def flip(a):
    return a.astype(F32).T.astype(BF16)


def remote(src, dst, send, recv, device):
    return pltpu.make_async_remote_copy(
        src_ref=src, dst_ref=dst, send_sem=send, recv_sem=recv, device_id=device, device_id_type=MESH
    )


class Exchange:
    def __init__(self, place, src, dst, mid, slot, send, recv, onward_device, direct):
        self.yh, self.xx, self.me, self.res = place
        self.src, self.dst, self.mid, self.slot = src, dst, mid, slot
        self.send, self.recv = send, recv
        self.onward_device, self.direct = onward_device, direct

    def near(self, k):
        to = self.yh * 4 + lax.rem(self.xx + 4 - k, 4)
        return remote(
            self.src.at[to], self.dst.at[self.slot, k],
            self.send.at[0, k], self.recv.at[0, k], (to, self.res),
        )

    def far(self, k):
        column = lax.rem(self.xx + 4 - k, 4)
        return remote(
            self.src.at[(1 - self.yh) * 4 + column], self.mid.at[k],
            self.send.at[1, k], self.recv.at[1, k], (self.yh * 4 + column, self.res),
        )

    def onward(self, k):
        column = self.xx
        src = self.mid.at[k]
        if k == 0 or self.direct:
            column = lax.rem(self.xx + 4 - k, 4)
            src = self.src.at[(1 - self.yh) * 4 + column]
        return remote(
            src, self.dst.at[self.slot, 4 + k], self.send.at[2, k], self.recv.at[2, k],
            ((1 - self.yh) * 4 + column, self.onward_device[1]),
        )

    def start(self):
        for k in (1, 3, 2):
            self.near(k).start()
        self.onward(0).start()
        for k in (1, 3, 2):
            if self.direct:
                self.onward(k).start()
            else:
                self.far(k).start()

    def forward(self):
        for k in () if self.direct else (1, 3, 2):
            self.far(k).wait_recv()
            self.onward(k).start()

    def arrived(self, place, pair, own):
        def wait(leg, k, t):
            spot = self.dst.at[place, t]
            remote(spot, spot, self.send.at[leg, k], self.recv.at[leg, k], self.onward_device).wait_recv()

        @pl.when(pair == 0)
        def _():
            own.wait()
            wait(0, 1, 1)

        @pl.when(pair == 1)
        def _():
            wait(0, 2, 2)
            wait(0, 3, 3)

        @pl.when(pair >= 2)
        def _():
            wait(2, 2 * pair - 4, 2 * pair)
            wait(2, 2 * pair - 3, 2 * pair + 1)

    def drain(self):
        for k in range(1, 4):
            self.near(k).wait_send()
            if not self.direct:
                self.far(k).wait_send()
        for k in range(4):
            self.onward(k).wait_send()


def swap_matrix():
    a = lax.broadcasted_iota(jnp.int32, (256, 256), 0)
    b = lax.broadcasted_iota(jnp.int32, (256, 256), 1)
    return jnp.where(b == ((a & 15) << 4) + (a >> 4), 1.0, 0.0).astype(BF16)


def pick_matrix(block, quarter):
    k = lax.broadcasted_iota(jnp.int32, (256, 256), 0) + block * 256
    n = lax.broadcasted_iota(jnp.int32, (256, 256), 1)
    same = ((k >> 7) == (n >> 5)) & (((k >> 5) & 3) == quarter) & ((k & 31) == (n & 31))
    return jnp.where(same, 1.0, 0.0).astype(BF16)


def kernel(
    x_in, wq_in, wk_in, wv_in, wg_in, wf_in, cq_in, ck_in, cv_in, cg_in, cf_in, ce_in, cs_in, out,
    x, wq, wk, wv, wg, wf, cq, ck, cv, cg, cf, ce, cs,
    normed, wt, ks, qs, vs, kmid, qmid, vmid, kz, vz, qg, logits, probs, stats,
    o_part, oc_s, oc_r, oy_s, oy_r, oa_s, oh, xc, gates, picks, osc,
    swap, x2, wide, done,
    ka_s, ka_r, qa_s, qa_r, va_s, va_r, kz_s, kz_r, vz_s, vz_r, qp_s, qp_r,
    st_s, st_r, oc_ss, oc_rs, oy_ss, oy_rs, oa_ss, oa_rs, col_s, col_r, back_s, back_r, own_s, load_s,
):
    me = lax.axis_index("seq")
    res = lax.axis_index("res")
    z = res // 4
    yl = lax.rem(res // 2, 2)
    c = lax.rem(res, 2)
    here = lax.rem(res, 4)
    yh = me // 4
    xx = lax.rem(me, 4)

    def at_res(zz, yy, cc):
        return (me, zz * 4 + yy * 2 + cc)

    z_up = lax.rem(z + 1, 4)
    z_down = lax.rem(z + 3, 4)
    z_far = lax.rem(z + 2, 4)
    up = at_res(z_up, yl, c)
    down = at_res(z_down, yl, c)
    twin = at_res(z, yl, 1 - c)
    beside = at_res(z, 1 - yl, c)
    across = at_res(z, 1 - yl, 1 - c)
    res_beside = z * 4 + (1 - yl) * 2 + c
    opposite = ((1 - yh) * 4 + xx, res)
    here_twin = yl * 2 + (1 - c)
    here_beside = (1 - yl) * 2 + c
    here_across = (1 - yl) * 2 + (1 - c)

    def diagonal(k):
        return ((1 - yh) * 4 + lax.rem(xx + 4 - k, 4), res_beside)

    def pair_of(u):
        return pl.ds(u * 2, 2)

    def turn(t):
        return lax.rem(me + t, SEQ_DEVICES)

    def unturn(t):
        return lax.rem(me + SEQ_DEVICES - t, SEQ_DEVICES)

    barrier = pltpu.get_barrier_semaphore()
    partners = [(turn(t), res) for t in range(1, SEQ_DEVICES)] + [up, down, twin, beside, across]
    partners += [diagonal(k) for k in range(4)]
    for device in partners:
        pl.semaphore_signal(barrier, inc=1, device_id=device, device_id_type=MESH)

    loads = [
        pltpu.make_async_copy(source, target, load_s.at[i])
        for i, (source, target) in enumerate(
            (
                (x_in, x), (wk_in, wk), (wq_in, wq), (wv_in, wv), (wg_in, wg), (wf_in, wf), (cq_in, cq),
                (ck_in, ck), (cv_in, cv), (cg_in, cg), (cf_in, cf), (ce_in, ce), (cs_in, cs),
            )
        )
    ]
    for load in loads:
        load.start()
    loads[1].wait()
    wt[0:256, :] = flip(wk[...])
    loads[0].wait()

    @pl.loop(0, 4)
    def _(quad):
        rows = pl.ds(pl.multiple_of(quad * 512, 512), 512)
        entries = x[pl.ds(quad * 4, 4)].reshape(512, 256)
        part = layer_normalize(entries.astype(F32)).astype(BF16)
        normed[rows, :] = part
        keys = matmul_nt(wt[0:256, :], part).astype(BF16)
        for h in range(HEADS):
            for s in range(4):
                place = pl.ds(pl.multiple_of(quad * 128 + 32 * s, 32), 32)
                ks[h, place, :] = keys[32 * h : 32 * h + 32, 128 * s : 128 * s + 128]

    pl.semaphore_wait(barrier, len(partners))

    place = (yh, xx, me, res)
    ka = Exchange(place, ks, kz, kmid, z, ka_s, ka_r, opposite, True)
    va = Exchange(place, vs, vz, vmid, z, va_s, va_r, opposite, False)
    qa = Exchange(place, qs, qg, qmid, here, qa_s, qa_r, diagonal(0), False)

    own_k = pltpu.make_async_copy(ks.at[me], kz.at[z, 0], own_s.at[0])
    own_q = pltpu.make_async_copy(qs.at[me], qg.at[here, 0], own_s.at[1])
    own_v = pltpu.make_async_copy(vs.at[me], vz.at[z, 0], own_s.at[2])
    own_k.start()
    ka.start()

    for load in loads[2:]:
        load.wait()
    wt[256:512, :] = flip(wq[...])
    wt[512:768, :] = flip(wv[...])

    def project(quad, first, target):
        rows = pl.ds(pl.multiple_of(quad * 512, 512), 512)
        turned = matmul_nt(wt[first : first + 256, :], normed[rows, :])
        lanes = pl.ds(pl.multiple_of(quad * 128, 128), 128)
        for h in range(HEADS):
            block = turned[32 * h : 32 * h + 32, :]
            stack = jnp.concatenate([block[:, 128 * s : 128 * s + 128] for s in range(4)], axis=0)
            target[h, :, lanes] = stack.T.astype(BF16)

    def ring_copy(buf, send, recv, way, source, device, u):
        spot = buf.at[source, pair_of(u)]
        return remote(spot, spot, send.at[way, u], recv.at[way, u], device)

    def ring(buf, send, recv, u):
        return (
            ring_copy(buf, send, recv, 0, z, up, u),
            ring_copy(buf, send, recv, 1, z, down, u),
        )

    def onward_up(buf, send, recv, u):
        return ring_copy(buf, send, recv, 2, z_down, up, u)

    def onward_down(buf, send, recv, u):
        return ring_copy(buf, send, recv, 2, z_up, down, u)

    def far_arrived(buf, send, recv, u):
        ring_copy(buf, send, recv, 2, z_far, up, u).wait_recv()

    def ring_forward(buf, send, recv, u):
        @pl.when(lax.rem(u, 2) == 0)
        def _():
            ring_copy(buf, send, recv, 0, z_down, up, u).wait_recv()
            onward_up(buf, send, recv, u).start()
            ring_copy(buf, send, recv, 1, z_up, down, u).wait_recv()

        @pl.when(lax.rem(u, 2) == 1)
        def _():
            ring_copy(buf, send, recv, 1, z_up, down, u).wait_recv()
            onward_down(buf, send, recv, u).start()
            ring_copy(buf, send, recv, 0, z_down, up, u).wait_recv()

    kzs = (kz, kz_s, kz_r)
    vzs = (vz, vz_s, vz_r)

    def first_place(u):
        half = u // 2
        return here * (1 - half) + here_beside * half

    def second_place(u):
        half = u // 2
        return here_beside * (1 - half) + here * half

    def q_copy(way, place, device, u):
        spot = qg.at[place, pair_of(u)]
        return remote(spot, spot, qp_s.at[way, u], qp_r.at[way, u], device)

    def q_twin(u):
        return q_copy(0, first_place(u), twin, u)

    def q_beside(u):
        return q_copy(1, first_place(u), beside, u)

    def q_onward(u):
        return q_copy(2, second_place(u), twin, u)

    def q_peers(u):
        qa.arrived(first_place(u), u, own_q)
        q_beside(u).start()
        q_twin(u).start()

    def q_forward(u):
        q_copy(1, second_place(u), beside, u).wait_recv()
        q_onward(u).start()

    def add_chunk(u):
        far_arrived(*kzs, u)
        half = u // 2
        q_copy(0, here_twin * (1 - half) + here_across * half, twin, u).wait_recv()
        q_copy(2, here_across * (1 - half) + here_twin * half, twin, u).wait_recv()
        keys = [
            jnp.concatenate([kz[zz, 2 * u + i] for zz in range(4)], axis=1) for i in range(2)
        ]
        for p in range(4):
            rows = slice(128 * p, 128 * p + 128)
            term = matmul(qg[p, 2 * u], keys[0]) + matmul(qg[p, 2 * u + 1], keys[1])

            @pl.when(u == 0)
            def _():
                logits[rows, :] = term

            @pl.when(u > 0)
            def _():
                logits[rows, :] += term

    scale = 1.0 / math.sqrt(SEQ_DEVICES * 16 * HEAD_DIM)

    def stat_copy(i, device):
        return remote(stats.at[here], stats.at[here], st_s.at[i], st_r.at[i], device)

    def stat_wait(i, spot):
        remote(stats.at[spot], stats.at[spot], st_s.at[i], st_r.at[i], twin).wait_recv()

    def local_softmax():
        for p in range(4):
            rows = slice(128 * p, 128 * p + 128)
            highest = jnp.max(logits[rows, :], axis=1, keepdims=True)
            expo = jnp.exp((logits[rows, :] - highest) * scale)
            logits[rows, :] = expo
            total = jnp.sum(expo, axis=1, keepdims=True)
            stats[here, 0, :, rows] = jnp.broadcast_to(highest, (128, 128)).T[0:8, :]
            stats[here, 1, :, rows] = jnp.broadcast_to(total, (128, 128)).T[0:8, :]
        stat_copy(1, beside).start()
        stat_copy(2, across).start()
        stat_copy(0, twin).start()

    def finish_softmax():
        stat_wait(0, here_twin)
        stat_wait(1, here_beside)
        stat_wait(2, here_across)
        highest = stats[0, 0]
        for p in range(1, 4):
            highest = jnp.maximum(highest, stats[p, 0])
        total = jnp.zeros((8, 512), F32)
        for p in range(4):
            total += stats[p, 1] * jnp.exp((stats[p, 0] - highest) * scale)
        factor = jnp.exp((stats[here, 0] - highest) * scale) / total
        for p in range(4):
            rows = slice(128 * p, 128 * p + 128)
            column = jnp.broadcast_to(factor[0:1, rows], (128, 128)).T
            for q in range(4):
                lanes = slice(128 * q, 128 * q + 128)
                probs[rows, lanes] = (logits[rows, lanes] * column).astype(BF16)

    def oc(t):
        return remote(oc_s.at[t], oc_r.at[t], oc_ss.at[t], oc_rs.at[t], twin)

    def oy(t):
        return remote(oy_s.at[t], oy_r.at[t], oy_ss.at[t], oy_rs.at[t], beside)

    def attend(u):
        far_arrived(*vzs, u)

        @pl.loop(0, 2)
        def _(i):
            t = 2 * u + i
            slot = t
            values = jnp.concatenate([vz[zz, t] for zz in range(4)], axis=0)
            for p in range(4):
                o_part[slot, p] = matmul(probs[128 * p : 128 * p + 128, :], values)
            for y in range(2):
                oc_s[t, y] = o_part[slot, 2 * y + 1 - c].astype(BF16)
            oc(t).start()

    same = pl.ds(pl.multiple_of(yh * 64, 64), 64)
    other = pl.ds(pl.multiple_of((1 - yh) * 64, 64), 64)

    def add_twin(u):
        @pl.loop(0, 2)
        def _(i):
            t = 2 * u + i
            slot = t
            oc(t).wait_recv()
            oy_s[t, 0] = (
                o_part[slot, here, other, :] + oc_r[t, yl, other, :].astype(F32)
            ).astype(BF16)
            oy_s[t, 1] = (
                o_part[slot, here_beside, same, :] + oc_r[t, 1 - yl, same, :].astype(F32)
            ).astype(BF16)
            oy(t).start()

    def column_rows(k):
        column = lax.rem(xx + 4 - k, 4)
        return column, pl.ds(pl.multiple_of(column * 16, 16), 16)

    def oa_near(t, k):
        column, rows = column_rows(k)
        return remote(
            oa_s.at[0, t, rows, :], oh.at[me, t], oa_ss.at[t, k], oa_rs.at[t, k], (yh * 4 + column, res)
        )

    def oa_far(t, k):
        rows = column_rows(k)[1]
        return remote(
            oa_s.at[1, t, rows, :], oh.at[me, t], oa_ss.at[t, 4 + k], oa_rs.at[t, 4 + k], diagonal(k)
        )

    def oa_wait(t, k):
        for far in (0, 1):
            if k == 0 and far == 0:
                continue
            source = lax.rem(yh + far, 2) * 4 + lax.rem(xx + k, 4)
            spot = oh.at[source, t]
            remote(spot, spot, oa_ss.at[t, 4 * far + k], oa_rs.at[t, 4 * far + k], beside).wait_recv()

    def add_beside(u):
        @pl.loop(0, 2)
        def _(i):
            t = 2 * u + i
            slot = t
            oy(t).wait_recv()
            oa_s[1, t] = (
                o_part[slot, here_beside, other, :]
                + oc_r[t, 1 - yl, other, :].astype(F32)
                + oy_r[t, 0].astype(F32)
            ).astype(BF16)
            for k in (2, 1, 3, 0):
                oa_far(t, k).start()
            oa_s[0, t] = (
                o_part[slot, here, same, :]
                + oc_r[t, yl, same, :].astype(F32)
                + oy_r[t, 1].astype(F32)
            ).astype(BF16)
            for k in (2, 1, 3):
                oa_near(t, k).start()
            oh[me, t] = oa_s[0, t, column_rows(0)[1], :]

    mine = pl.ds(pl.multiple_of(me * 16, 16), 16)
    own_x = pltpu.make_async_copy(x.at[:, mine, :], xc.at[mine], own_s.at[3])

    def x_copy(t):
        g = turn(t)
        return remote(
            x.at[:, pl.ds(pl.multiple_of(g * 16, 16), 16), :], xc.at[mine],
            col_s.at[t], col_r.at[t], (g, res),
        )

    def x_start():
        own_x.start()
        for t in range(1, SEQ_DEVICES):
            x_copy(t).start()

    def x_arrived():
        own_x.wait()
        for t in range(1, SEQ_DEVICES):
            spot = xc.at[pl.ds(pl.multiple_of(unturn(t) * 16, 16), 16)]
            remote(spot, spot, col_s.at[t], col_r.at[t], (turn(t), res)).wait_recv()

    def gate_block(i):
        rows = pl.ds(pl.multiple_of(i * 512, 512), 512)
        entries = xc[pl.ds(pl.multiple_of(i * 32, 32), 32)].reshape(512, 256).astype(F32)
        gates[rows, :] = jax.nn.sigmoid(matmul(layer_normalize(entries).astype(BF16), wg[...]))

    def prepare(i):
        @pl.when(i == 0)
        def _():
            wt[0:256, :] = flip(cq[...])
            swap[...] = swap_matrix()

        @pl.when(i == 1)
        def _():
            wt[256:512, :] = flip(cv[...])
            wt[512:768, :] = flip(cg[...])

        for quarter in range(4):
            picks[quarter, pl.ds(pl.multiple_of(i * 256, 256), 256), :] = pick_matrix(i, quarter)
        wide[i] = jnp.zeros((256, 1024), BF16)

    @pl.loop(0, 4)
    def _(quad):
        project(quad, 256, qs)

    own_q.start()
    qa.start()

    def v_project(u):
        project(2 * u, 512, vs)
        project(2 * u + 1, 512, vs)

        @pl.when(u == 1)
        def _():
            own_v.start()
            va.start()

    def k_own(u):
        ka.arrived(z, u, own_k)
        for copy in ring(*kzs, u):
            copy.start()

    def v_own(u):
        va.arrived(z, u, own_v)
        for copy in ring(*vzs, u):
            copy.start()

    @pl.loop(0, 13)
    def _(tick):
        def during(first, action, count=4):
            @pl.when((tick >= first) & (tick < first + count))
            def _():
                action(tick - first)

        during(0, k_own)
        during(1, lambda u: ka.forward(), 1)
        during(1, v_project, 2)
        during(3, v_own)
        during(1, lambda u: ring_forward(*kzs, u))
        during(5, lambda u: ring_forward(*vzs, u))
        during(2, lambda u: qa.forward(), 1)
        during(4, lambda u: va.forward(), 1)
        during(1, q_peers)
        during(2, q_forward)
        during(2, prepare, 4)
        during(6, lambda u: x_start(), 1)
        during(3, add_chunk)
        during(6, lambda u: local_softmax(), 1)
        during(7, lambda u: finish_softmax(), 1)
        during(8, add_twin)
        during(7, attend)
        during(9, add_beside)
        during(9, lambda u: x_arrived(), 1)
        during(9, gate_block, 4)

    @pl.loop(0, 8)
    def _(t):
        for k in range(4):
            oa_wait(t, k)

    def chunk_of(h, g):
        return (g // 4 - h // 4) % 2 * 4 + (g - h) % 4

    @pl.loop(0, 4)
    def _(quarter):
        stack = jnp.concatenate(
            [
                jnp.concatenate(
                    [
                        jnp.concatenate(
                            [oh[h, chunk_of(h, g), :, 128 * q : 128 * q + 128] for g in range(8)], axis=0
                        )
                        for h in range(HEADS)
                    ],
                    axis=1,
                )
                for q in range(4)
            ],
            axis=0,
        )
        spread = matmul(stack, picks[quarter]).astype(BF16)
        for q in range(4):
            osc[:, 4 * q + quarter] = spread[128 * q : 128 * q + 128, :].reshape(8, 16, 256)

    @pl.loop(0, 8, unroll=4)
    def _(g):
        rows = pl.ds(pl.multiple_of(g * 256, 256), 256)
        update = (gates[rows, :] * osc[g].reshape(256, 256).astype(F32)).astype(BF16)
        entries = xc[pl.ds(pl.multiple_of(g * 16, 16), 16)].reshape(256, 256).astype(F32)
        after = (entries + matmul(update, wf[...])).astype(BF16)
        turned = matmul(swap[...], after).astype(BF16)
        for r in range(16):
            x2[pl.ds(pl.multiple_of(r * 128 + g * 16, 16), 16), :] = turned[16 * r : 16 * r + 16, :]

    col_scale = 1.0 / math.sqrt(HEAD_DIM)

    def result(block, t):
        g = turn(t)
        return remote(
            done.at[pl.ds(block * 4, 4), pl.ds(pl.multiple_of(g * 16, 16), 16), :],
            out.at[pl.ds(me * 16 + block * 4, 4)],
            back_s.at[block, t], back_r.at[block, t], (g, res),
        )

    @pl.loop(0, 4)
    def _(block):
        rows = pl.ds(pl.multiple_of(block * 512, 512), 512)
        entries = x2[rows, :].astype(F32)
        part = layer_normalize(entries).astype(BF16)
        keys = matmul(part, ck[...]).astype(BF16)
        turned = matmul_nt(wt[...], part)
        queries = turned[0:256, :].astype(BF16)
        values = turned[256:512, :].astype(BF16)
        gate = jax.nn.sigmoid(turned[512:768, :])
        updates = []
        for r in range(4):
            lanes = slice(128 * r, 128 * r + 128)
            for h in range(HEADS):
                wide[r, 32 * h : 32 * h + 32, 128 * h : 128 * h + 128] = queries[
                    32 * h : 32 * h + 32, lanes
                ]
            scores = matmul(keys[lanes, :], wide[r])
            highest = jnp.max(scores, axis=0, keepdims=True)
            expo = jnp.exp((scores - highest) * col_scale)
            total = jnp.sum(expo, axis=0, keepdims=True)
            weights = (expo * (1.0 / total)).astype(BF16)
            mixed = []
            for h in range(0, HEADS, 2):
                both = matmul(values[32 * h : 32 * h + 64, lanes], weights[:, 128 * h : 128 * h + 256])
                mixed += [both[0:32, 0:128], both[32:64, 128:256]]
            mixed = jnp.concatenate(mixed, axis=0)
            updates.append((gate[:, lanes] * mixed).astype(BF16).astype(F32).T.astype(BF16))
        update = jnp.concatenate(updates, axis=0)
        after = (entries + matmul(update, cf[...])).astype(BF16).astype(F32)
        hidden = matmul(layer_normalize(after).astype(BF16), ce[...])
        hidden = jnp.maximum(hidden, 0.0).astype(BF16)
        total = (after + matmul(hidden, cs[...])).astype(BF16)
        for r in range(4):
            done[block * 4 + r] = total[128 * r : 128 * r + 128, :]
        for t in range(1, SEQ_DEVICES):
            result(block, t).start()

    out[pl.ds(pl.multiple_of(me * 16, 16), 16)] = done[:, mine, :]

    for exchange in (ka, qa, va):
        exchange.drain()
    stat_copy(0, twin).wait_send()
    stat_copy(1, beside).wait_send()
    stat_copy(2, across).wait_send()

    @pl.loop(0, 4)
    def _(u):
        for buf in (kzs, vzs):
            for copy in ring(*buf, u):
                copy.wait_send()

            @pl.when(lax.rem(u, 2) == 0)
            def _():
                onward_up(*buf, u).wait_send()

            @pl.when(lax.rem(u, 2) == 1)
            def _():
                onward_down(*buf, u).wait_send()

        q_twin(u).wait_send()
        q_beside(u).wait_send()
        q_onward(u).wait_send()

    @pl.loop(0, 8)
    def _(t):
        oc(t).wait_send()
        oy(t).wait_send()
        for k in range(4):
            oa_far(t, k).wait_send()
        for k in range(1, 4):
            oa_near(t, k).wait_send()

    for t in range(1, SEQ_DEVICES):
        x_copy(t).wait_send()

    @pl.loop(1, 8)
    def _(t):
        g = unturn(t)
        for block in range(4):
            spot = out.at[pl.ds(g * 16 + block * 4, 4)]
            remote(spot, spot, back_s.at[block, t], back_r.at[block, t], (turn(t), res)).wait_recv()

    @pl.loop(1, 8)
    def _(t):
        for block in range(4):
            result(block, t).wait_send()


def on_device(
    homolog_tensor,
    horizontal_probe_matrix,
    horizontal_lookup_matrix,
    horizontal_payload_matrix,
    horizontal_sigmoid_matrix,
    horizontal_final_matrix,
    vertical_probe_matrix,
    vertical_lookup_matrix,
    vertical_payload_matrix,
    vertical_sigmoid_matrix,
    vertical_final_matrix,
    expanding_matrix,
    shrinking_matrix,
):
    dma = pltpu.SemaphoreType.DMA
    vmem = pltpu.VMEM
    columns = pl.pallas_call(
        kernel,
        name="msa_block",
        out_shape=jax.ShapeDtypeStruct((128, 16, 256), BF16),
        in_specs=[pl.BlockSpec(memory_space=pl.ANY)] * 13,
        out_specs=pl.BlockSpec(memory_space=vmem),
        scratch_shapes=[vmem((16, 128, 256), BF16)]
        + [vmem((256, 256), BF16)] * 10
        + [vmem((256, 1024), BF16), vmem((1024, 256), BF16)]
        + [
            vmem((2048, 256), BF16),
            vmem((768, 256), BF16),
            vmem((8, 512, 128), BF16),
            vmem((8, 128, 512), BF16),
            vmem((8, 128, 512), BF16),
            vmem((4, 512, 128), BF16),
            vmem((4, 128, 512), BF16),
            vmem((4, 128, 512), BF16),
            vmem((4, 8, 512, 128), BF16),
            vmem((4, 8, 128, 512), BF16),
            vmem((4, 8, 128, 512), BF16),
            vmem((512, 512), F32),
            vmem((512, 512), BF16),
            vmem((4, 2, 8, 512), F32),
            vmem((8, 4, 128, 512), F32),
            vmem((8, 2, 128, 512), BF16),
            vmem((8, 2, 128, 512), BF16),
            vmem((8, 2, 64, 512), BF16),
            vmem((8, 2, 64, 512), BF16),
            vmem((2, 8, 64, 512), BF16),
            vmem((8, 8, 16, 512), BF16),
            vmem((128, 16, 256), BF16),
            vmem((2048, 256), F32),
            vmem((4, 1024, 256), BF16),
            vmem((8, 16, 16, 256), BF16),
            vmem((256, 256), BF16),
            vmem((2048, 256), BF16),
            vmem((4, 256, 1024), BF16),
            vmem((16, 128, 256), BF16),
        ]
        + [dma((3, 4))] * 6
        + [dma((3, 4))] * 6
        + [dma((3,))] * 2
        + [dma((8,))] * 4
        + [dma((8, 8))] * 2
        + [dma((8,))] * 2
        + [dma((4, 8))] * 2
        + [dma((4,))]
        + [dma((13,))],
        compiler_params=pltpu.CompilerParams(
            collective_id=0, has_side_effects=True, vmem_limit_bytes=62 * 2**20
        ),
    )(
        homolog_tensor,
        horizontal_probe_matrix,
        horizontal_lookup_matrix,
        horizontal_payload_matrix,
        horizontal_sigmoid_matrix,
        horizontal_final_matrix,
        vertical_probe_matrix,
        vertical_lookup_matrix,
        vertical_payload_matrix,
        vertical_sigmoid_matrix,
        vertical_final_matrix,
        expanding_matrix,
        shrinking_matrix,
    )
    return jnp.transpose(columns, (1, 0, 2))


def solution(mesh):
    in_specs = (P("seq", "res", None), P(), P(), P(), P(), P(), P(), P(), P(), P(), P(), P(), P())
    out_specs = P("seq", "res", None)
    return jax.shard_map(
        on_device, mesh=mesh, in_specs=in_specs, out_specs=out_specs, check_vma=False
    )
```

```python
import math

import jax
import jax.numpy as jnp
from jax import lax
from jax.experimental import pallas as pl
from jax.experimental.pallas import tpu as pltpu
from jax.sharding import PartitionSpec as P

HEADS = 8
HEAD_DIM = 32
SEQ_DEVICES = 8
MESH = pl.DeviceIdType.MESH
BF16 = jnp.bfloat16
F32 = jnp.float32
NT = (((1,), (1,)), ((), ()))


def layer_normalize(entries):
    center = entries - jnp.mean(entries, axis=-1, keepdims=True)
    spread = jnp.mean(center * center, axis=-1, keepdims=True)
    return center * lax.rsqrt(spread + 1e-05)


def matmul(a, b):
    return jnp.dot(a, b, preferred_element_type=F32)


def matmul_nt(a, b):
    return lax.dot_general(a, b, NT, preferred_element_type=F32)


def flip(a):
    return a.astype(F32).T.astype(BF16)


def remote(src, dst, send, recv, device):
    return pltpu.make_async_remote_copy(
        src_ref=src, dst_ref=dst, send_sem=send, recv_sem=recv, device_id=device, device_id_type=MESH
    )


class Exchange:
    def __init__(self, place, src, dst, mid, slot, send, recv, onward_device, direct):
        self.yh, self.xx, self.me, self.res = place
        self.src, self.dst, self.mid, self.slot = src, dst, mid, slot
        self.send, self.recv = send, recv
        self.onward_device, self.direct = onward_device, direct

    def near(self, k):
        to = self.yh * 4 + lax.rem(self.xx + 4 - k, 4)
        return remote(
            self.src.at[to], self.dst.at[self.slot, k],
            self.send.at[0, k], self.recv.at[0, k], (to, self.res),
        )

    def far(self, k):
        column = lax.rem(self.xx + 4 - k, 4)
        return remote(
            self.src.at[(1 - self.yh) * 4 + column], self.mid.at[k],
            self.send.at[1, k], self.recv.at[1, k], (self.yh * 4 + column, self.res),
        )

    def onward(self, k):
        column = self.xx
        src = self.mid.at[k]
        if k == 0 or self.direct:
            column = lax.rem(self.xx + 4 - k, 4)
            src = self.src.at[(1 - self.yh) * 4 + column]
        return remote(
            src, self.dst.at[self.slot, 4 + k], self.send.at[2, k], self.recv.at[2, k],
            ((1 - self.yh) * 4 + column, self.onward_device[1]),
        )

    def start(self):
        for k in (1, 3, 2):
            self.near(k).start()
        self.onward(0).start()
        for k in (1, 3, 2):
            if self.direct:
                self.onward(k).start()
            else:
                self.far(k).start()

    def forward(self):
        for k in () if self.direct else (1, 3, 2):
            self.far(k).wait_recv()
            self.onward(k).start()

    def arrived(self, place, pair, own):
        def wait(leg, k, t):
            spot = self.dst.at[place, t]
            remote(spot, spot, self.send.at[leg, k], self.recv.at[leg, k], self.onward_device).wait_recv()

        @pl.when(pair == 0)
        def _():
            own.wait()
            wait(0, 1, 1)

        @pl.when(pair == 1)
        def _():
            wait(0, 2, 2)
            wait(0, 3, 3)

        @pl.when(pair >= 2)
        def _():
            wait(2, 2 * pair - 4, 2 * pair)
            wait(2, 2 * pair - 3, 2 * pair + 1)

    def drain(self):
        for k in range(1, 4):
            self.near(k).wait_send()
            if not self.direct:
                self.far(k).wait_send()
        for k in range(4):
            self.onward(k).wait_send()


def swap_matrix():
    a = lax.broadcasted_iota(jnp.int32, (256, 256), 0)
    b = lax.broadcasted_iota(jnp.int32, (256, 256), 1)
    return jnp.where(b == ((a & 15) << 4) + (a >> 4), 1.0, 0.0).astype(BF16)


def pick_matrix(block, quarter):
    k = lax.broadcasted_iota(jnp.int32, (256, 256), 0) + block * 256
    n = lax.broadcasted_iota(jnp.int32, (256, 256), 1)
    same = ((k >> 7) == (n >> 5)) & (((k >> 5) & 3) == quarter) & ((k & 31) == (n & 31))
    return jnp.where(same, 1.0, 0.0).astype(BF16)


def kernel(
    x_in, wq_in, wk_in, wv_in, wg_in, wf_in, cq_in, ck_in, cv_in, cg_in, cf_in, ce_in, cs_in, out,
    x, wq, wk, wv, wg, wf, cq, ck, cv, cg, cf, ce, cs,
    normed, wt, ks, qs, vs, kmid, qmid, vmid, kz, vz, qg, logits, probs, stats, factors,
    o_part, oc_s, oc_r, oy_s, oy_r, oa_s, oh, xc, gates, picks, osc,
    swap, x2, wide, done,
    ka_s, ka_r, qa_s, qa_r, va_s, va_r, kz_s, kz_r, vz_s, vz_r, qp_s, qp_r,
    st_s, st_r, oc_ss, oc_rs, oy_ss, oy_rs, oa_ss, oa_rs, col_s, col_r, back_s, back_r, own_s, load_s,
):
    me = lax.axis_index("seq")
    res = lax.axis_index("res")
    z = res // 4
    yl = lax.rem(res // 2, 2)
    c = lax.rem(res, 2)
    here = lax.rem(res, 4)
    yh = me // 4
    xx = lax.rem(me, 4)

    def at_res(zz, yy, cc):
        return (me, zz * 4 + yy * 2 + cc)

    z_up = lax.rem(z + 1, 4)
    z_down = lax.rem(z + 3, 4)
    z_far = lax.rem(z + 2, 4)
    up = at_res(z_up, yl, c)
    down = at_res(z_down, yl, c)
    twin = at_res(z, yl, 1 - c)
    beside = at_res(z, 1 - yl, c)
    across = at_res(z, 1 - yl, 1 - c)
    res_beside = z * 4 + (1 - yl) * 2 + c
    opposite = ((1 - yh) * 4 + xx, res)
    here_twin = yl * 2 + (1 - c)
    here_beside = (1 - yl) * 2 + c
    here_across = (1 - yl) * 2 + (1 - c)

    def diagonal(k):
        return ((1 - yh) * 4 + lax.rem(xx + 4 - k, 4), res_beside)

    def pair_of(u):
        return pl.ds(u * 2, 2)

    def turn(t):
        return lax.rem(me + t, SEQ_DEVICES)

    def unturn(t):
        return lax.rem(me + SEQ_DEVICES - t, SEQ_DEVICES)

    barrier = pltpu.get_barrier_semaphore()
    partners = [(turn(t), res) for t in range(1, SEQ_DEVICES)] + [up, down, twin, beside, across]
    partners += [diagonal(k) for k in range(4)]
    for device in partners:
        pl.semaphore_signal(barrier, inc=1, device_id=device, device_id_type=MESH)

    loads = [
        pltpu.make_async_copy(source, target, load_s.at[i])
        for i, (source, target) in enumerate(
            (
                (x_in, x), (wk_in, wk), (wq_in, wq), (wv_in, wv), (wg_in, wg), (wf_in, wf), (cq_in, cq),
                (ck_in, ck), (cv_in, cv), (cg_in, cg), (cf_in, cf), (ce_in, ce), (cs_in, cs),
            )
        )
    ]
    for load in loads:
        load.start()
    loads[1].wait()
    wt[0:256, :] = flip(wk[...])
    loads[0].wait()

    @pl.loop(0, 4)
    def _(quad):
        rows = pl.ds(pl.multiple_of(quad * 512, 512), 512)
        entries = x[pl.ds(quad * 4, 4)].reshape(512, 256)
        part = layer_normalize(entries.astype(F32)).astype(BF16)
        normed[rows, :] = part
        keys = matmul_nt(wt[0:256, :], part).astype(BF16)
        for h in range(HEADS):
            for s in range(4):
                place = pl.ds(pl.multiple_of(quad * 128 + 32 * s, 32), 32)
                ks[h, place, :] = keys[32 * h : 32 * h + 32, 128 * s : 128 * s + 128]

    pl.semaphore_wait(barrier, len(partners))

    place = (yh, xx, me, res)
    ka = Exchange(place, ks, kz, kmid, z, ka_s, ka_r, opposite, True)
    va = Exchange(place, vs, vz, vmid, z, va_s, va_r, opposite, False)
    qa = Exchange(place, qs, qg, qmid, here, qa_s, qa_r, diagonal(0), False)

    own_k = pltpu.make_async_copy(ks.at[me], kz.at[z, 0], own_s.at[0])
    own_q = pltpu.make_async_copy(qs.at[me], qg.at[here, 0], own_s.at[1])
    own_v = pltpu.make_async_copy(vs.at[me], vz.at[z, 0], own_s.at[2])
    own_k.start()
    ka.start()

    for load in loads[2:]:
        load.wait()
    wt[256:512, :] = flip(wq[...])
    wt[512:768, :] = flip(wv[...])

    def project(quad, first, target):
        rows = pl.ds(pl.multiple_of(quad * 512, 512), 512)
        turned = matmul_nt(wt[first : first + 256, :], normed[rows, :])
        lanes = pl.ds(pl.multiple_of(quad * 128, 128), 128)
        for h in range(HEADS):
            block = turned[32 * h : 32 * h + 32, :]
            stack = jnp.concatenate([block[:, 128 * s : 128 * s + 128] for s in range(4)], axis=0)
            target[h, :, lanes] = stack.T.astype(BF16)

    def ring_copy(buf, send, recv, way, source, device, u):
        spot = buf.at[source, pair_of(u)]
        return remote(spot, spot, send.at[way, u], recv.at[way, u], device)

    def ring(buf, send, recv, u):
        return (
            ring_copy(buf, send, recv, 0, z, up, u),
            ring_copy(buf, send, recv, 1, z, down, u),
        )

    def onward_up(buf, send, recv, u):
        return ring_copy(buf, send, recv, 2, z_down, up, u)

    def onward_down(buf, send, recv, u):
        return ring_copy(buf, send, recv, 2, z_up, down, u)

    def far_arrived(buf, send, recv, u):
        ring_copy(buf, send, recv, 2, z_far, up, u).wait_recv()

    def ring_forward(buf, send, recv, u):
        @pl.when(lax.rem(u, 2) == 0)
        def _():
            ring_copy(buf, send, recv, 0, z_down, up, u).wait_recv()
            onward_up(buf, send, recv, u).start()
            ring_copy(buf, send, recv, 1, z_up, down, u).wait_recv()

        @pl.when(lax.rem(u, 2) == 1)
        def _():
            ring_copy(buf, send, recv, 1, z_up, down, u).wait_recv()
            onward_down(buf, send, recv, u).start()
            ring_copy(buf, send, recv, 0, z_down, up, u).wait_recv()

    kzs = (kz, kz_s, kz_r)
    vzs = (vz, vz_s, vz_r)

    def first_place(u):
        half = u // 2
        return here * (1 - half) + here_beside * half

    def second_place(u):
        half = u // 2
        return here_beside * (1 - half) + here * half

    def q_copy(way, place, device, u):
        spot = qg.at[place, pair_of(u)]
        return remote(spot, spot, qp_s.at[way, u], qp_r.at[way, u], device)

    def q_twin(u):
        return q_copy(0, first_place(u), twin, u)

    def q_beside(u):
        return q_copy(1, first_place(u), beside, u)

    def q_onward(u):
        return q_copy(2, second_place(u), twin, u)

    def q_peers(u):
        qa.arrived(first_place(u), u, own_q)
        q_beside(u).start()
        q_twin(u).start()

    def q_forward(u):
        q_copy(1, second_place(u), beside, u).wait_recv()
        q_onward(u).start()

    def add_chunk(u):
        far_arrived(*kzs, u)
        half = u // 2
        q_copy(0, here_twin * (1 - half) + here_across * half, twin, u).wait_recv()
        q_copy(2, here_across * (1 - half) + here_twin * half, twin, u).wait_recv()
        keys = [
            jnp.concatenate([kz[zz, 2 * u + i] for zz in range(4)], axis=1) for i in range(2)
        ]
        for p in range(4):
            rows = slice(128 * p, 128 * p + 128)
            term = matmul(qg[p, 2 * u], keys[0]) + matmul(qg[p, 2 * u + 1], keys[1])

            @pl.when(u == 0)
            def _():
                logits[rows, :] = term

            @pl.when(u > 0)
            def _():
                logits[rows, :] += term

    scale = 1.0 / math.sqrt(SEQ_DEVICES * 16 * HEAD_DIM)

    def stat_copy(i, device):
        return remote(stats.at[here], stats.at[here], st_s.at[i], st_r.at[i], device)

    def stat_wait(i, spot):
        remote(stats.at[spot], stats.at[spot], st_s.at[i], st_r.at[i], twin).wait_recv()

    def local_softmax():
        for p in range(4):
            rows = slice(128 * p, 128 * p + 128)
            highest = jnp.max(logits[rows, :], axis=1, keepdims=True)
            expo = jnp.exp((logits[rows, :] - highest) * scale)
            probs[rows, :] = expo.astype(BF16)
            total = jnp.sum(expo, axis=1, keepdims=True)
            stats[here, 0, :, rows] = jnp.broadcast_to(highest, (128, 128)).T[0:8, :]
            stats[here, 1, :, rows] = jnp.broadcast_to(total, (128, 128)).T[0:8, :]
        stat_copy(1, beside).start()
        stat_copy(2, across).start()
        stat_copy(0, twin).start()

    def finish_softmax():
        stat_wait(0, here_twin)
        stat_wait(1, here_beside)
        stat_wait(2, here_across)
        highest = stats[0, 0]
        for p in range(1, 4):
            highest = jnp.maximum(highest, stats[p, 0])
        total = jnp.zeros((8, 512), F32)
        for p in range(4):
            total += stats[p, 1] * jnp.exp((stats[p, 0] - highest) * scale)
        factor = jnp.exp((stats[here, 0] - highest) * scale) / total
        for p in range(4):
            rows = slice(128 * p, 128 * p + 128)
            factors[p] = jnp.broadcast_to(factor[0:1, rows], (128, 128)).T

    def scaled(slot, p, rows):
        factor = factors[p, rows, :]
        return o_part[slot, p, rows, :] * jnp.concatenate([factor] * 4, axis=1)

    def oc(t):
        return remote(oc_s.at[t], oc_r.at[t], oc_ss.at[t], oc_rs.at[t], twin)

    def oy(t):
        return remote(oy_s.at[t], oy_r.at[t], oy_ss.at[t], oy_rs.at[t], beside)

    def attend(u):
        far_arrived(*vzs, u)

        @pl.loop(0, 2)
        def _(i):
            t = 2 * u + i
            slot = t
            values = jnp.concatenate([vz[zz, t] for zz in range(4)], axis=0)
            for p in range(4):
                o_part[slot, p] = matmul(probs[128 * p : 128 * p + 128, :], values)

        @pl.when(u == 0)
        def _():
            finish_softmax()

        @pl.loop(0, 2)
        def _(i):
            t = 2 * u + i
            for y in range(2):
                oc_s[t, y] = scaled(t, 2 * y + 1 - c, slice(None)).astype(BF16)
            oc(t).start()

    same = pl.ds(pl.multiple_of(yh * 64, 64), 64)
    other = pl.ds(pl.multiple_of((1 - yh) * 64, 64), 64)

    def add_twin(u):
        @pl.loop(0, 2)
        def _(i):
            t = 2 * u + i
            slot = t
            oc(t).wait_recv()
            oy_s[t, 0] = (
                scaled(slot, here, other) + oc_r[t, yl, other, :].astype(F32)
            ).astype(BF16)
            oy_s[t, 1] = (
                scaled(slot, here_beside, same) + oc_r[t, 1 - yl, same, :].astype(F32)
            ).astype(BF16)
            oy(t).start()

    def column_rows(k):
        column = lax.rem(xx + 4 - k, 4)
        return column, pl.ds(pl.multiple_of(column * 16, 16), 16)

    def oa_near(t, k):
        column, rows = column_rows(k)
        return remote(
            oa_s.at[0, t, rows, :], oh.at[me, t], oa_ss.at[t, k], oa_rs.at[t, k], (yh * 4 + column, res)
        )

    def oa_far(t, k):
        rows = column_rows(k)[1]
        return remote(
            oa_s.at[1, t, rows, :], oh.at[me, t], oa_ss.at[t, 4 + k], oa_rs.at[t, 4 + k], diagonal(k)
        )

    def oa_wait(t, k):
        for far in (0, 1):
            if k == 0 and far == 0:
                continue
            source = lax.rem(yh + far, 2) * 4 + lax.rem(xx + k, 4)
            spot = oh.at[source, t]
            remote(spot, spot, oa_ss.at[t, 4 * far + k], oa_rs.at[t, 4 * far + k], beside).wait_recv()

    def add_beside(u):
        @pl.loop(0, 2)
        def _(i):
            t = 2 * u + i
            slot = t
            oy(t).wait_recv()
            oa_s[1, t] = (
                scaled(slot, here_beside, other)
                + oc_r[t, 1 - yl, other, :].astype(F32)
                + oy_r[t, 0].astype(F32)
            ).astype(BF16)
            for k in (2, 1, 3, 0):
                oa_far(t, k).start()
            oa_s[0, t] = (
                scaled(slot, here, same)
                + oc_r[t, yl, same, :].astype(F32)
                + oy_r[t, 1].astype(F32)
            ).astype(BF16)
            for k in (2, 1, 3):
                oa_near(t, k).start()
            oh[me, t] = oa_s[0, t, column_rows(0)[1], :]

    mine = pl.ds(pl.multiple_of(me * 16, 16), 16)
    own_x = pltpu.make_async_copy(x.at[:, mine, :], xc.at[mine], own_s.at[3])

    def x_copy(t):
        g = turn(t)
        return remote(
            x.at[:, pl.ds(pl.multiple_of(g * 16, 16), 16), :], xc.at[mine],
            col_s.at[t], col_r.at[t], (g, res),
        )

    def x_start():
        own_x.start()
        for t in range(1, SEQ_DEVICES):
            x_copy(t).start()

    def x_arrived():
        own_x.wait()
        for t in range(1, SEQ_DEVICES):
            spot = xc.at[pl.ds(pl.multiple_of(unturn(t) * 16, 16), 16)]
            remote(spot, spot, col_s.at[t], col_r.at[t], (turn(t), res)).wait_recv()

    def gate_block(i):
        rows = pl.ds(pl.multiple_of(i * 512, 512), 512)
        entries = xc[pl.ds(pl.multiple_of(i * 32, 32), 32)].reshape(512, 256).astype(F32)
        gates[rows, :] = jax.nn.sigmoid(matmul(layer_normalize(entries).astype(BF16), wg[...]))

    def prepare(i):
        @pl.when(i == 0)
        def _():
            wt[0:256, :] = flip(cq[...])
            swap[...] = swap_matrix()

        @pl.when(i == 1)
        def _():
            wt[256:512, :] = flip(cv[...])
            wt[512:768, :] = flip(cg[...])

        for quarter in range(4):
            picks[quarter, pl.ds(pl.multiple_of(i * 256, 256), 256), :] = pick_matrix(i, quarter)
        wide[i] = jnp.zeros((256, 1024), BF16)

    @pl.loop(0, 4)
    def _(quad):
        project(quad, 256, qs)

    own_q.start()
    qa.start()

    def v_project(u):
        project(2 * u, 512, vs)
        project(2 * u + 1, 512, vs)

        @pl.when(u == 1)
        def _():
            own_v.start()
            va.start()

    def k_own(u):
        ka.arrived(z, u, own_k)
        for copy in ring(*kzs, u):
            copy.start()

    def v_own(u):
        va.arrived(z, u, own_v)
        for copy in ring(*vzs, u):
            copy.start()

    @pl.loop(0, 12)
    def _(tick):
        def during(first, action, count=4):
            @pl.when((tick >= first) & (tick < first + count))
            def _():
                action(tick - first)

        during(0, k_own)
        during(1, lambda u: ka.forward(), 1)
        during(1, v_project, 2)
        during(3, v_own)
        during(1, lambda u: ring_forward(*kzs, u))
        during(5, lambda u: ring_forward(*vzs, u))
        during(2, lambda u: qa.forward(), 1)
        during(4, lambda u: va.forward(), 1)
        during(1, q_peers)
        during(2, q_forward)
        during(2, prepare, 4)
        during(6, lambda u: x_start(), 1)
        during(3, add_chunk)
        during(6, lambda u: local_softmax(), 1)
        during(7, add_twin)
        during(6, attend)
        during(8, add_beside)
        during(8, lambda u: x_arrived(), 1)
        during(8, gate_block, 4)

    @pl.loop(0, 8)
    def _(t):
        for k in range(4):
            oa_wait(t, k)

    def chunk_of(h, g):
        return (g // 4 - h // 4) % 2 * 4 + (g - h) % 4

    @pl.loop(0, 4)
    def _(quarter):
        stack = jnp.concatenate(
            [
                jnp.concatenate(
                    [
                        jnp.concatenate(
                            [oh[h, chunk_of(h, g), :, 128 * q : 128 * q + 128] for g in range(8)], axis=0
                        )
                        for h in range(HEADS)
                    ],
                    axis=1,
                )
                for q in range(4)
            ],
            axis=0,
        )
        spread = matmul(stack, picks[quarter]).astype(BF16)
        for q in range(4):
            osc[:, 4 * q + quarter] = spread[128 * q : 128 * q + 128, :].reshape(8, 16, 256)

    @pl.loop(0, 8, unroll=8)
    def _(g):
        rows = pl.ds(pl.multiple_of(g * 256, 256), 256)
        update = (gates[rows, :] * osc[g].reshape(256, 256).astype(F32)).astype(BF16)
        entries = xc[pl.ds(pl.multiple_of(g * 16, 16), 16)].reshape(256, 256).astype(F32)
        after = (entries + matmul(update, wf[...])).astype(BF16)
        turned = matmul(swap[...], after).astype(BF16)
        for r in range(16):
            x2[pl.ds(pl.multiple_of(r * 128 + g * 16, 16), 16), :] = turned[16 * r : 16 * r + 16, :]

    col_scale = 1.0 / math.sqrt(HEAD_DIM)

    def result(block, t):
        g = turn(t)
        return remote(
            done.at[pl.ds(block * 4, 4), pl.ds(pl.multiple_of(g * 16, 16), 16), :],
            out.at[pl.ds(me * 16 + block * 4, 4)],
            back_s.at[block, t], back_r.at[block, t], (g, res),
        )

    @pl.loop(0, 4)
    def _(block):
        rows = pl.ds(pl.multiple_of(block * 512, 512), 512)
        entries = x2[rows, :].astype(F32)
        part = layer_normalize(entries).astype(BF16)
        keys = matmul(part, ck[...]).astype(BF16)
        turned = matmul_nt(wt[...], part)
        queries = turned[0:256, :].astype(BF16)
        values = turned[256:512, :].astype(BF16)
        gate = jax.nn.sigmoid(turned[512:768, :])
        updates = []
        for r in range(4):
            lanes = slice(128 * r, 128 * r + 128)
            for h in range(HEADS):
                wide[r, 32 * h : 32 * h + 32, 128 * h : 128 * h + 128] = queries[
                    32 * h : 32 * h + 32, lanes
                ]
            scores = matmul(keys[lanes, :], wide[r])
            highest = jnp.max(scores, axis=0, keepdims=True)
            expo = jnp.exp((scores - highest) * col_scale)
            total = jnp.sum(expo, axis=0, keepdims=True)
            weights = (expo * (1.0 / total)).astype(BF16)
            mixed = []
            for h in range(0, HEADS, 2):
                both = matmul(values[32 * h : 32 * h + 64, lanes], weights[:, 128 * h : 128 * h + 256])
                mixed += [both[0:32, 0:128], both[32:64, 128:256]]
            mixed = jnp.concatenate(mixed, axis=0)
            updates.append((gate[:, lanes] * mixed).astype(BF16).astype(F32).T.astype(BF16))
        update = jnp.concatenate(updates, axis=0)
        after = (entries + matmul(update, cf[...])).astype(BF16).astype(F32)
        hidden = matmul(layer_normalize(after).astype(BF16), ce[...])
        hidden = jnp.maximum(hidden, 0.0).astype(BF16)
        total = (after + matmul(hidden, cs[...])).astype(BF16)
        for r in range(4):
            done[block * 4 + r] = total[128 * r : 128 * r + 128, :]
        for t in range(1, SEQ_DEVICES):
            result(block, t).start()

    out[pl.ds(pl.multiple_of(me * 16, 16), 16)] = done[:, mine, :]

    for exchange in (ka, qa, va):
        exchange.drain()
    stat_copy(0, twin).wait_send()
    stat_copy(1, beside).wait_send()
    stat_copy(2, across).wait_send()

    @pl.loop(0, 4)
    def _(u):
        for buf in (kzs, vzs):
            for copy in ring(*buf, u):
                copy.wait_send()

            @pl.when(lax.rem(u, 2) == 0)
            def _():
                onward_up(*buf, u).wait_send()

            @pl.when(lax.rem(u, 2) == 1)
            def _():
                onward_down(*buf, u).wait_send()

        q_twin(u).wait_send()
        q_beside(u).wait_send()
        q_onward(u).wait_send()

    @pl.loop(0, 8)
    def _(t):
        oc(t).wait_send()
        oy(t).wait_send()
        for k in range(4):
            oa_far(t, k).wait_send()
        for k in range(1, 4):
            oa_near(t, k).wait_send()

    for t in range(1, SEQ_DEVICES):
        x_copy(t).wait_send()

    @pl.loop(1, 8)
    def _(t):
        g = unturn(t)
        for block in range(4):
            spot = out.at[pl.ds(g * 16 + block * 4, 4)]
            remote(spot, spot, back_s.at[block, t], back_r.at[block, t], (turn(t), res)).wait_recv()

    @pl.loop(1, 8)
    def _(t):
        for block in range(4):
            result(block, t).wait_send()


def on_device(
    homolog_tensor,
    horizontal_probe_matrix,
    horizontal_lookup_matrix,
    horizontal_payload_matrix,
    horizontal_sigmoid_matrix,
    horizontal_final_matrix,
    vertical_probe_matrix,
    vertical_lookup_matrix,
    vertical_payload_matrix,
    vertical_sigmoid_matrix,
    vertical_final_matrix,
    expanding_matrix,
    shrinking_matrix,
):
    dma = pltpu.SemaphoreType.DMA
    vmem = pltpu.VMEM
    columns = pl.pallas_call(
        kernel,
        name="msa_block",
        out_shape=jax.ShapeDtypeStruct((128, 16, 256), BF16),
        in_specs=[pl.BlockSpec(memory_space=pl.ANY)] * 13,
        out_specs=pl.BlockSpec(memory_space=vmem),
        scratch_shapes=[vmem((16, 128, 256), BF16)]
        + [vmem((256, 256), BF16)] * 10
        + [vmem((256, 1024), BF16), vmem((1024, 256), BF16)]
        + [
            vmem((2048, 256), BF16),
            vmem((768, 256), BF16),
            vmem((8, 512, 128), BF16),
            vmem((8, 128, 512), BF16),
            vmem((8, 128, 512), BF16),
            vmem((4, 512, 128), BF16),
            vmem((4, 128, 512), BF16),
            vmem((4, 128, 512), BF16),
            vmem((4, 8, 512, 128), BF16),
            vmem((4, 8, 128, 512), BF16),
            vmem((4, 8, 128, 512), BF16),
            vmem((512, 512), F32),
            vmem((512, 512), BF16),
            vmem((4, 2, 8, 512), F32),
            vmem((4, 128, 128), F32),
            vmem((8, 4, 128, 512), F32),
            vmem((8, 2, 128, 512), BF16),
            vmem((8, 2, 128, 512), BF16),
            vmem((8, 2, 64, 512), BF16),
            vmem((8, 2, 64, 512), BF16),
            vmem((2, 8, 64, 512), BF16),
            vmem((8, 8, 16, 512), BF16),
            vmem((128, 16, 256), BF16),
            vmem((2048, 256), F32),
            vmem((4, 1024, 256), BF16),
            vmem((8, 16, 16, 256), BF16),
            vmem((256, 256), BF16),
            vmem((2048, 256), BF16),
            vmem((4, 256, 1024), BF16),
            vmem((16, 128, 256), BF16),
        ]
        + [dma((3, 4))] * 6
        + [dma((3, 4))] * 6
        + [dma((3,))] * 2
        + [dma((8,))] * 4
        + [dma((8, 8))] * 2
        + [dma((8,))] * 2
        + [dma((4, 8))] * 2
        + [dma((4,))]
        + [dma((13,))],
        compiler_params=pltpu.CompilerParams(
            collective_id=0, has_side_effects=True, vmem_limit_bytes=62 * 2**20
        ),
    )(
        homolog_tensor,
        horizontal_probe_matrix,
        horizontal_lookup_matrix,
        horizontal_payload_matrix,
        horizontal_sigmoid_matrix,
        horizontal_final_matrix,
        vertical_probe_matrix,
        vertical_lookup_matrix,
        vertical_payload_matrix,
        vertical_sigmoid_matrix,
        vertical_final_matrix,
        expanding_matrix,
        shrinking_matrix,
    )
    return jnp.transpose(columns, (1, 0, 2))


def solution(mesh):
    in_specs = (P("seq", "res", None), P(), P(), P(), P(), P(), P(), P(), P(), P(), P(), P(), P())
    out_specs = P("seq", "res", None)
    return jax.shard_map(
        on_device, mesh=mesh, in_specs=in_specs, out_specs=out_specs, check_vma=False
    )
```
